32 devices in a mesh: wide: 16 (over z, y, x), narrow: 2 (over core).
Axes of the slice: x: 2, y: 2, z: 4, core: 2. Of those that a mesh axis runs over, the one named last changes fastest.
Arguments:
- frames: bfloat16 [16384, 1024], P(('wide', 'narrow')), may hold values from -6 to 6
- segment_ids: int32 [16, 1024], P('wide'), may hold values from 0 to 5, never falling along the last dimension, each value on 1 to 350 neighbouring positions
- w_query: bfloat16 [1024, 1024], P(None, 'narrow'), may hold values from -0.25 to 0.25
- w_key: bfloat16 [1024, 1024], P(None, 'narrow'), may hold values from -0.25 to 0.25
- w_value: bfloat16 [1024, 1024], P(None, 'narrow'), may hold values from -0.1875 to 0.1875
- w_out: bfloat16 [1024, 1024], P('narrow'), may hold values from -0.5 to 0.5
- w_gate: bfloat16 [1024, 4096], P(None, 'narrow'), may hold values from -0.1875 to 0.1875
- w_up: bfloat16 [1024, 4096], P(None, 'narrow'), may hold values from -0.1875 to 0.1875
- w_down: bfloat16 [4096, 1024], P('narrow'), may hold values from -0.09375 to 0.09375
- norm1_gain: float32 [1024], replicated, may hold values from 0.1 to 1.9
- norm1_bias: float32 [1024], replicated, may hold values from -3 to 3
- norm2_gain: float32 [1024], replicated, may hold values from 0.1 to 1.9
- norm2_bias: float32 [1024], replicated, may hold values from -3 to 3
- scale_attn: float32 [1024], replicated, may hold values from 0.5 to 1.5
- scale_mlp: float32 [1024], replicated, may hold values from 0.5 to 1.5
- output_grad: bfloat16 [16384, 1024], P(('wide', 'narrow')), may hold values from -6 to 6
Outputs:
- output: bfloat16 [16384, 1024], P(('wide', 'narrow'))
- input_grad: bfloat16 [16384, 1024], P(('wide', 'narrow'))
- query_grad: float32 [1024, 1024], P('wide', 'narrow')
- key_grad: float32 [1024, 1024], P('wide', 'narrow')
- value_grad: float32 [1024, 1024], P('wide', 'narrow')
- out_proj_grad: float32 [1024, 1024], P('narrow', 'wide')
- gate_grad: float32 [1024, 4096], P('wide', 'narrow')
- up_grad: float32 [1024, 4096], P('wide', 'narrow')
- down_grad: float32 [4096, 1024], P('narrow', 'wide')
- norm1_gain_grad: float32 [1024], replicated
- norm1_bias_grad: float32 [1024], replicated
- norm2_gain_grad: float32 [1024], replicated
- norm2_bias_grad: float32 [1024], replicated
- scale_attn_grad: float32 [1024], replicated
- scale_mlp_grad: float32 [1024], replicated
The draws below stay inside these ranges and needn't reach their ends.
Inputs may be any that keep to these rules, and one draw needn't show every extreme that they name: `segment_ids`: along each sequence the clip numbers never fall, and a clip holds at most 350 frames.
All inputs are finite; a program needn't handle non-finite values.
Results may differ from the reference program's by a relative error of at most 0.023.
Values may be sent and summed in bfloat16 or wider, within the bound.
No kernel may reach another device: no remote copies, remote signals or barrier semaphores. Data moves between devices by JAX's collectives and lax.ppermute only.
A program may use at most 192 MiB of HBM per device.

```python
import math
import jax
import jax.numpy as jnp
import numpy as np
from jax import lax

D = 1024
HEADS = 16
HEAD_DIM = 64
FF = 4096
WINDOW = 128
LEN = 1024
SEQS = 16
TOKENS = 16384


def with_spikes(drawn, key, source, target, blocks, factor):
    owner, partner = [(jnp.arange(drawn.shape[dim]) // (drawn.shape[dim] // blocks)).reshape([-1 if axis == dim else 1 for axis in range(drawn.ndim)]) for dim in (source, target)]
    chosen = jax.random.permutation(key, blocks)[partner]
    strong = (owner == chosen) | (owner == (partner + blocks // 2) % blocks)
    return jnp.where(strong, factor * drawn, drawn)


def block_scale(rng, extent, split, least, largest):
    def one(position, parts):
        steps = jax.random.uniform(jax.random.fold_in(jax.random.fold_in(rng, 6), position), (parts,), jnp.float32, least / len(split), largest / len(split))
        return jnp.repeat(jnp.exp(steps), extent[position] // parts).reshape((-1,) + (1,) * (len(extent) - position - 1))

    loudness = one(*split[0])
    for cut in split[1:]:
        loudness = loudness * one(*cut)
    return loudness


def profile(amount, total, bound, slope):
    portions = [(1 << 20) // math.isqrt(standing ** slope) + 1 for standing in range(2, amount + 1)]
    surplus, counts = total - bound - (amount - 1), [1] * (amount - 1)
    while surplus > 0:
        free = [i for i in range(amount - 1) if counts[i] < bound]
        mass, budget = sum([portions[i] for i in free]), surplus
        for i in free:
            extra = min(bound - counts[i], max(1, budget * portions[i] // mass), surplus)
            counts[i] = counts[i] + extra
            surplus = surplus - extra
    return np.array([bound] + counts)


def uneven(own_key, number_of, total, bound, lean):
    if number_of == 2:
        one = jax.random.randint(own_key, (), max(1, total - bound), min(bound, total - 1) + 1)
        return jnp.stack([one, total - one])
    lengths = jnp.asarray(profile(number_of, total, bound, lean), jnp.int32)
    twos = (number_of - 1) // 2
    giver, taker = lengths[1:1 + 2 * twos:2], lengths[2:2 + 2 * twos:2]
    slack = jnp.minimum(giver - 1, bound - taker)
    shifted = jax.random.randint(jax.random.fold_in(own_key, 1), (twos,), 0, 1 << 20) % (slack + 1)
    lengths = lengths.at[1:1 + 2 * twos:2].set(giver - shifted).at[2:2 + 2 * twos:2].set(taker + shifted)
    return lengths[jax.random.permutation(jax.random.fold_in(own_key, 2), number_of)]


def bell_draw(stream_key, shape, spread, bound, cuts=(), held_as=jnp.bfloat16):
    loudness = block_scale(stream_key, shape, cuts, -0.22, 0.18) if cuts else 1.0
    entries = jax.random.normal(stream_key, shape, jnp.float32) * spread * loudness
    return jnp.minimum(jnp.maximum(entries, -bound), bound).astype(held_as)


def gaussian_with(stream_key, shape, deviation, bound, cuts, heavy, kind=jnp.bfloat16):
    values = deviation * jax.random.normal(stream_key, shape, jnp.float32)
    if cuts:
        values = values * block_scale(stream_key, shape, cuts, -0.22, 0.18)
    return jnp.clip(with_spikes(values, jax.random.fold_in(stream_key, 3), *heavy), -bound, bound).astype(kind)


def setup_inputs(seed: int = 0) -> dict:
    streams_of = jax.random.split(jax.random.key(seed), 17)
    frames = bell_draw(streams_of[0], (TOKENS, D), 1.0, 6.0, ((0, 32),))
    segment_ids = jax.vmap(lambda own: jnp.searchsorted(jnp.cumsum(uneven(own, LEN // 256 + 2, LEN, min(350, LEN - 1), 0)), jnp.arange(LEN), side="right"))(jax.random.split(streams_of[1], SEQS)).reshape((SEQS, LEN)).astype(jnp.int32)
    w_query = bell_draw(streams_of[2], (D, D), (D // 2) ** -0.5, 0.25, ((1, 2),))
    w_key = bell_draw(streams_of[3], (D, D), (D // 2) ** -0.5, 0.25, ((1, 2),))
    w_value = bell_draw(streams_of[4], (D, D), D ** -0.5, 0.1875, ((1, 2),))
    w_out = bell_draw(streams_of[5], (D, D), (D // 8) ** -0.5, 0.5, ((0, 2),))
    w_gate = bell_draw(streams_of[6], (D, FF), D ** -0.5, 0.1875, ((1, 2),))
    w_up = bell_draw(streams_of[7], (D, FF), D ** -0.5, 0.1875, ((1, 2),))
    w_down = bell_draw(streams_of[8], (FF, D), FF ** -0.5, 0.09375, ((0, 2),))
    norm1_gain = jnp.clip(1.0 + 0.18 * jax.random.normal(streams_of[9], (D,), jnp.float32), 0.1, 1.9)
    norm1_bias = bell_draw(streams_of[10], (D,), 0.3, 3.0, (), jnp.float32)
    norm2_gain = jnp.clip(1.0 + 0.18 * jax.random.normal(streams_of[11], (D,), jnp.float32), 0.1, 1.9)
    norm2_bias = bell_draw(streams_of[12], (D,), 0.3, 3.0, (), jnp.float32)
    scale_attn = jnp.clip(jax.random.uniform(streams_of[13], (D,), jnp.float32, 0.5, 1.5), 0.5, 1.5)
    scale_mlp = jnp.clip(jax.random.uniform(streams_of[14], (D,), jnp.float32, 0.5, 1.5), 0.5, 1.5)
    output_grad = gaussian_with(streams_of[15], (TOKENS, D), 1.0, 6.0, ((0, 32),), (0, 1, 32, 2.75))
    return dict(frames=frames, segment_ids=segment_ids, w_query=w_query, w_key=w_key, w_value=w_value, w_out=w_out, w_gate=w_gate, w_up=w_up, w_down=w_down, norm1_gain=norm1_gain, norm1_bias=norm1_bias, norm2_gain=norm2_gain, norm2_bias=norm2_bias, scale_attn=scale_attn, scale_mlp=scale_mlp, output_grad=output_grad)


norm_eps = 1e-05
masked_score = -1e+30
highest = lax.Precision.HIGHEST

@jax.custom_vjp
def low(v):
    return lax.optimization_barrier(v.astype(jnp.bfloat16)).astype(jnp.float32)

@jax.custom_vjp
def low_back(v):
    return v

def low_keep(v):
    return (low(v), None)

def low_pass(kept, grad):
    return (grad,)

def back_keep(v):
    return (v, None)

def back_low(kept, grad):
    return (low(grad),)
low.defvjp(low_keep, low_pass)
low_back.defvjp(back_keep, back_low)

def layer_norm(row_block, norm_gain, norm_shift):
    mean_row = lax.optimization_barrier(jnp.mean(row_block, axis=-1, keepdims=True))
    centred = row_block - mean_row
    inverse = lax.rsqrt(lax.optimization_barrier(jnp.mean(centred * centred, axis=-1, keepdims=True)) + norm_eps)
    return centred * inverse * norm_gain + norm_shift

def positions(segment_ids):
    place = lax.broadcasted_iota(jnp.int32, segment_ids.shape, 1)
    edges = jnp.concatenate([jnp.ones_like(segment_ids[:, :1]), (segment_ids[:, 1:] != segment_ids[:, :-1]).astype(jnp.int32)], axis=1)
    starts = lax.cummax(jnp.where(edges == 1, place, 0), axis=1)
    return (place - starts).astype(jnp.float32)

def rotary_tables(where_in, half_size):
    frequency = jnp.exp(jnp.arange(half_size, dtype=jnp.float32) * (-math.log(10000.0) / half_size))
    angles = where_in.reshape(-1, 1) * frequency[None, :]
    return (jnp.cos(angles)[:, None, :], jnp.sin(angles)[:, None, :])

def rotate(vectors, cosine_table, sine_table):
    half_size = vectors.shape[-1] // 2
    front_half = vectors[..., :half_size]
    back_half = vectors[..., half_size:]
    return jnp.concatenate([front_half * cosine_table - back_half * sine_table, front_half * sine_table + back_half * cosine_table], axis=-1)

def attend(pieces):
    query_rows, key_rows, value_rows, segment = pieces
    score_scale = query_rows.shape[-1] ** (-0.5)
    scores = jnp.einsum('qhd,khd->hqk', query_rows, key_rows, precision=highest)
    scores = low_back(scores * score_scale)
    place = lax.iota(jnp.int32, query_rows.shape[0])
    offset = place[None, :] - place[:, None]
    allowed = (offset >= -(WINDOW // 2)) & (offset < WINDOW // 2) & (segment[:, None] == segment[None, :])
    weights = low(jax.nn.softmax(jnp.where(allowed[None], scores, masked_score), axis=-1))
    return jnp.einsum('hqk,khd->qhd', weights, value_rows, precision=highest)

def layer(frames, w_query, w_key, w_value, w_out, w_gate, w_up, w_down, norm1_gain, norm1_bias, norm2_gain, norm2_bias, scale_attn, scale_mlp, cosine_table, sine_table, segment_ids):
    row_count = frames.shape[0]
    normed = low(layer_norm(frames, norm1_gain, norm1_bias))

    def heads_of(matrix):
        return matrix.reshape(row_count, HEADS, HEAD_DIM)
    query_rows = low(rotate(heads_of(low_back(jnp.dot(normed, w_query, precision=highest))), cosine_table, sine_table))
    key_rows = low(rotate(heads_of(low_back(jnp.dot(normed, w_key, precision=highest))), cosine_table, sine_table))
    value_rows = heads_of(low(low_back(jnp.dot(normed, w_value, precision=highest))))
    shape_four = (SEQS, LEN, HEADS, HEAD_DIM)
    mixture = lax.map(jax.checkpoint(attend), (query_rows.reshape(shape_four), key_rows.reshape(shape_four), value_rows.reshape(shape_four), segment_ids))
    mixture = low(low_back(mixture.reshape(row_count, D)))
    attn_out = low_back(jnp.dot(mixture, w_out, precision=highest))
    middle = frames + scale_attn * attn_out
    normed_two = low(layer_norm(middle, norm2_gain, norm2_bias))
    gate_pre = low_back(jnp.dot(normed_two, w_gate, precision=highest))
    up_pre = low_back(jnp.dot(normed_two, w_up, precision=highest))
    hidden = low(jax.nn.silu(gate_pre) * up_pre)
    mlp_out = low_back(jnp.dot(hidden, w_down, precision=highest))
    return middle + scale_mlp * mlp_out

def reference(frames, segment_ids, w_query, w_key, w_value, w_out, w_gate, w_up, w_down, norm1_gain, norm1_bias, norm2_gain, norm2_bias, scale_attn, scale_mlp, output_grad):
    floats = [array.astype(jnp.float32) for array in (frames, w_query, w_key, w_value, w_out, w_gate, w_up, w_down, norm1_gain, norm1_bias, norm2_gain, norm2_bias, scale_attn, scale_mlp)]
    cosine_table, sine_table = rotary_tables(positions(segment_ids), HEAD_DIM // 2)

    def forward(*params):
        return layer(*params, cosine_table, sine_table, segment_ids)
    result, pullback = jax.vjp(forward, *floats)
    gradients = pullback(output_grad.astype(jnp.float32))
    return (result.astype(jnp.bfloat16), gradients[0].astype(jnp.bfloat16), gradients[1], gradients[2], gradients[3], gradients[4], gradients[5], gradients[6], gradients[7], gradients[8], gradients[9], gradients[10], gradients[11], gradients[12], gradients[13])
```

```python
import functools
import math

import jax
import jax.numpy as jnp
import numpy as np
from jax import lax
from jax.experimental import pallas as pl
from jax.experimental.pallas import tpu as pltpu
from jax.sharding import PartitionSpec as P

HEAD_DIM = 64
HALF_WINDOW = 64
CLIPS = 6
MAX_CLIP = 384
norm_eps = 1e-05
masked_score = -1e30
bf16 = jnp.bfloat16
f32 = jnp.float32
NN = (((1,), (0,)), ((), ()))
NT = (((1,), (1,)), ((), ()))
TN = (((0,), (0,)), ((), ()))


def dot(a, b, dims=NN):
    return lax.dot_general(a, b, dims, preferred_element_type=f32)


def call(body, name, grid, in_specs, out_specs, out_shape, scratch=(), prefetch=0, mib=48):
    return pl.pallas_call(
        body,
        grid_spec=pltpu.PrefetchScalarGridSpec(
            num_scalar_prefetch=prefetch,
            grid=grid,
            in_specs=in_specs,
            out_specs=out_specs,
            scratch_shapes=list(scratch),
        ),
        out_shape=out_shape,
        compiler_params=pltpu.CompilerParams(vmem_limit_bytes=mib * 2**20),
        name=name,
    )


def whole(shape):
    return pl.BlockSpec(
        shape, lambda *_: (0,) * len(shape), pipeline_mode=pl.Buffered(1)
    )


def like(shape, kind=bf16):
    return jax.ShapeDtypeStruct(shape, kind)


def normalise(rows):
    centred = rows - jnp.mean(rows, axis=-1, keepdims=True)
    inverse = lax.rsqrt(jnp.mean(centred * centred, axis=-1, keepdims=True) + norm_eps)
    return centred * inverse, inverse


def norm_back(incoming, unit, inverse, gain):
    scaled = incoming * gain
    return inverse * (
        scaled
        - jnp.mean(scaled, axis=-1, keepdims=True)
        - unit * jnp.mean(scaled * unit, axis=-1, keepdims=True)
    )


def rope_table():
    half = HEAD_DIM // 2
    lane = np.arange(128)
    frequency = np.exp((lane % half) * (-math.log(10000.0) / half))
    angle = np.arange(MAX_CLIP)[:, None] * frequency[None, :]
    sign = np.where(lane % HEAD_DIM < half, -1.0, 1.0)
    parts = []
    for table in (np.cos(angle), np.sin(angle) * sign):
        high = table.astype(np.float32).astype(bf16)
        parts += [high, (table - high.astype(np.float64)).astype(np.float32).astype(bf16)]
    return np.concatenate(parts, axis=1)


def swap_halves(values):
    half = HEAD_DIM // 2
    width = values.shape[-1]
    lane = lax.broadcasted_iota(jnp.int32, values.shape, 1)
    return jnp.where(
        lane % HEAD_DIM < half,
        pltpu.roll(values, width - half, 1),
        pltpu.roll(values, half, 1),
    )


def column_of(row, start, count):
    pieces = []
    for place in range(count // 128):
        piece = row[:, pl.ds(pl.multiple_of(start + place * 128, 128), 128)]
        pieces.append(jnp.broadcast_to(piece.astype(f32), (128, 128)).T)
    return jnp.concatenate(pieces, axis=0) if len(pieces) > 1 else pieces[0]


def project_body(core, own, other, seg, gain, bias, table, wq, wk, wv, q, k, v, u, x, cos, sin, *, own_blocks, blocks):
    step = pl.program_id(0)
    block = lax.rem(step + core[0] * own_blocks, blocks)
    rows_per = own.shape[0]
    raw = jnp.where(step < own_blocks, own[...], other[...])
    x[...] = raw
    unit, _ = normalise(raw.astype(f32))
    normed = (unit * gain[...] + bias[...]).astype(bf16)
    u[...] = normed
    ids = seg[...]
    mine = column_of(seg, block * rows_per, rows_per)
    start = jnp.zeros_like(mine)
    for clip in range(CLIPS - 1):
        count = jnp.sum((ids == clip).astype(f32), axis=-1, keepdims=True)
        start += jnp.where(mine > clip, count, 0.0)
    place = lax.broadcasted_iota(jnp.int32, mine.shape, 0) + block * rows_per
    place = place - start.astype(jnp.int32)
    lane = lax.broadcasted_iota(jnp.int32, mine.shape, 1)
    hot = jnp.concatenate(
        [(place == lane + 128 * part).astype(bf16) for part in range(MAX_CLIP // 128)], axis=1
    )
    rows = dot(hot, table[...])
    cosine = rows[:, :128] + rows[:, 128:256]
    sine = rows[:, 256:384] + rows[:, 384:]
    cos[...] = cosine
    sin[...] = sine

    def turned(weights):
        flat = dot(normed, weights)
        return [
            flat[:, at : at + 128] * cosine + swap_halves(flat[:, at : at + 128]) * sine
            for at in range(0, flat.shape[1], 128)
        ]

    for pair, values in enumerate(turned(wq[...])):
        q[:, pair * 128 : pair * 128 + 128] = (values * HEAD_DIM**-0.5).astype(bf16)
    for pair, values in enumerate(turned(wk[...])):
        k[:, pair * 128 : pair * 128 + 128] = values.astype(bf16)
    v[...] = dot(normed, wv[...]).astype(bf16)


def project(core, pieces, seg, gain, bias, wq, wk, wv, rows_per=256):
    own, other = pieces if len(pieces) == 2 else (pieces[0], pieces[0])
    own_blocks = own.shape[0] // rows_per
    length, width = own.shape[0] * len(pieces), own.shape[1]
    blocks = length // rows_per
    heads = wq.shape[1]

    def out(columns):
        return pl.BlockSpec(
            (rows_per, columns), lambda i, core: (lax.rem(i + core[0] * own_blocks, blocks), 0)
        )

    table = rope_table()
    return call(
        functools.partial(project_body, own_blocks=own_blocks, blocks=blocks),
        "project",
        (blocks,),
        [
            pl.BlockSpec((rows_per, width), lambda i, core: (jnp.minimum(i, own_blocks - 1), 0)),
            pl.BlockSpec(
                (rows_per, width),
                lambda i, core: (jnp.maximum(i - own_blocks, 0) if len(pieces) == 2 else 0, 0),
            ),
            whole(seg.shape),
            whole((1, width)),
            whole((1, width)),
            whole(table.shape),
            whole(wq.shape),
            whole(wk.shape),
            whole(wv.shape),
        ],
        [out(heads)] * 3 + [out(width)] * 2 + [out(128)] * 2,
        [like((length, heads))] * 3 + [like((length, width))] * 2 + [like((length, 128), f32)] * 2,
        prefetch=1,
    )(core, own, other, seg, gain, bias, jnp.asarray(table), wq, wk, wv)


def band(seg, block, rows_per, span, length):
    first = block * rows_per
    start = jnp.clip(first - HALF_WINDOW, 0, length - span)
    return first, pl.multiple_of(start, HALF_WINDOW)


def two_heads(values):
    lane = lax.broadcasted_iota(jnp.int32, values.shape, 1)
    zero = jnp.zeros_like(values)
    return jnp.concatenate(
        [jnp.where(lane < HEAD_DIM, values, zero), jnp.where(lane < HEAD_DIM, zero, values)], axis=0
    )


def one_each(stacked):
    count = stacked.shape[0] // 2
    lane = lax.broadcasted_iota(jnp.int32, (count, 128), 1)
    return jnp.where(lane < HEAD_DIM, stacked[:count], stacked[count:])


def attend_body(q, k, v, seg, segw, o, weights, *, offset, span):
    rows_per = q.shape[0]
    length = k.shape[0]
    block = pl.program_id(0) + offset
    first, start = band(seg, block, rows_per, span, length)
    mine = column_of(seg, first, rows_per)
    theirs = segw[pl.ds(lax.div(start, HALF_WINDOW), 1), :]
    gap = (
        lax.broadcasted_iota(jnp.int32, (rows_per, span), 1)
        - lax.broadcasted_iota(jnp.int32, (rows_per, span), 0)
        + (start - first)
    )
    mine_wide = jnp.concatenate([mine] * (span // 128), axis=1)
    allowed = (gap >= -HALF_WINDOW) & (gap < HALF_WINDOW) & (mine_wide == theirs.astype(f32))
    penalty = jnp.where(allowed, 0.0, masked_score)
    penalty = jnp.concatenate([penalty, penalty], axis=0)
    for pair in range(q.shape[1] // 128):
        lanes = slice(pair * 128, pair * 128 + 128)
        keys = k[pl.ds(start, span), lanes]
        values = v[pl.ds(start, span), lanes]
        scores = dot(two_heads(q[:, lanes]), keys, NT) + penalty
        lifted = jnp.exp(scores - jnp.max(scores, axis=-1, keepdims=True))
        chances = (lifted * (1.0 / jnp.sum(lifted, axis=-1, keepdims=True))).astype(bf16)
        weights[0, pair] = chances
        o[:, lanes] = one_each(dot(chances, values)).astype(bf16)


def windows(seg, span):
    length = seg.shape[1]
    return jnp.concatenate(
        [
            seg[:, min(at, length - span) : min(at, length - span) + span]
            for at in range(0, length, HALF_WINDOW)
        ],
        axis=0,
    )


def attend(q, k, v, seg, segw, offset, blocks, rows_per, span):
    length, heads = q.shape
    pairs = heads // 128
    return call(
        functools.partial(attend_body, offset=offset, span=span),
        "attend",
        (blocks,),
        [
            pl.BlockSpec((rows_per, heads), lambda i: (i + offset, 0)),
            whole(k.shape),
            whole(v.shape),
            whole(seg.shape),
            whole(segw.shape),
        ],
        [
            pl.BlockSpec((rows_per, heads), lambda i: (i, 0)),
            pl.BlockSpec((1, pairs, 2 * rows_per, span), lambda i: (i, 0, 0, 0)),
        ],
        [like((blocks * rows_per, heads)), like((blocks, pairs, 2 * rows_per, span))],
    )(q, k, v, seg, segw)


def attend_back_body(go, q, k, v, wa, wb, cos, sin, gq, gk, gv, acc_k, acc_v, *, span, half_blocks):
    rows_per = q.shape[0]
    length = k.shape[0]
    block = pl.program_id(0)
    _, start = band(None, block, rows_per, span, length)

    @pl.when(block == 0)
    def _():
        acc_k[...] = jnp.zeros_like(acc_k)
        acc_v[...] = jnp.zeros_like(acc_v)

    mine = pl.ds(pl.multiple_of(block * rows_per, rows_per), rows_per)
    cosine, sine = cos[mine, :], sin[mine, :]
    keys_at = pl.ds(start, span)
    for pair in range(q.shape[1] // 128):
        lanes = slice(pair * 128, pair * 128 + 128)
        keys = k[keys_at, lanes]
        values = v[keys_at, lanes]
        chances = jnp.where(block < half_blocks, wa[0, pair], wb[0, pair])
        full = chances.astype(f32)
        go_two = two_heads(go[:, lanes])
        change = dot(go_two, values, NT)
        weighted = jnp.sum(full * change, axis=-1, keepdims=True)
        gs = (full * (change - weighted)).astype(bf16)
        gq_rows = one_each(dot(gs, keys)) * HEAD_DIM**-0.5
        gq[:, lanes] = (gq_rows * cosine - swap_halves(gq_rows) * sine).astype(bf16)
        acc_k[keys_at, lanes] += dot(gs, two_heads(q[:, lanes]), TN)
        acc_v[keys_at, lanes] += dot(chances, go_two, TN)

    @pl.when(block == pl.num_programs(0) - 1)
    def _():
        gv[...] = acc_v[...].astype(bf16)
        for pair in range(q.shape[1] // 128):
            lanes = slice(pair * 128, pair * 128 + 128)
            rows = acc_k[:, lanes]
            gk[:, lanes] = (rows * cos[...] - swap_halves(rows) * sin[...]).astype(bf16)


def attend_back(go, q, k, v, wa, wb, cos, sin, rows_per, span):
    length, heads = q.shape
    pairs = heads // 128
    blocks = length // rows_per
    half = blocks // 2
    row = pl.BlockSpec((rows_per, heads), lambda i: (i, 0))
    chance = (1, pairs, 2 * rows_per, span)
    return call(
        functools.partial(attend_back_body, span=span, half_blocks=half),
        "attend_back",
        (blocks,),
        [
            row,
            row,
            whole(k.shape),
            whole(v.shape),
            pl.BlockSpec(chance, lambda i: (jnp.minimum(i, half - 1), 0, 0, 0)),
            pl.BlockSpec(chance, lambda i: (jnp.maximum(i - half, 0), 0, 0, 0)),
            whole(cos.shape),
            whole(sin.shape),
        ],
        [row, whole(k.shape), whole(k.shape)],
        [like((length, heads))] * 3,
        scratch=[pltpu.VMEM((length, heads), f32)] * 2,
    )(go, q, k, v, wa, wb, cos, sin)


def put_transposed(target, places, values, at, piece):
    for group in range(values.shape[1] // 128):
        turned = values[:, group * 128 : group * 128 + 128].T
        for part in range(128 // piece):
            place = places[group * (128 // piece) + part]
            target[pl.ds(pl.multiple_of(place * piece, piece), piece), at] = turned[
                part * piece : part * piece + piece
            ]


def cotangent_body(core, places, own, other, scale, dy, gm, gmt, *, own_blocks, blocks, piece):
    step = pl.program_id(0)
    raw = jnp.where(step < own_blocks, own[...], other[...])
    dy[...] = raw
    scaled = (raw.astype(f32) * scale[...]).astype(bf16)
    gm[...] = scaled
    put_transposed(gmt, places, scaled, slice(None), piece)


def cotangent(core, places, pieces, scale, piece, rows_per=256):
    own, other = pieces if len(pieces) == 2 else (pieces[0], pieces[0])
    own_blocks = own.shape[0] // rows_per
    length, width = own.shape[0] * len(pieces), own.shape[1]
    blocks = length // rows_per

    def at(i, core):
        return lax.rem(i + core[0] * own_blocks, blocks)

    row = pl.BlockSpec((rows_per, width), lambda i, core, places: (at(i, core), 0))
    return call(
        functools.partial(cotangent_body, own_blocks=own_blocks, blocks=blocks, piece=piece),
        "cotangent",
        (blocks,),
        [
            pl.BlockSpec(
                (rows_per, width), lambda i, core, places: (jnp.minimum(i, own_blocks - 1), 0)
            ),
            pl.BlockSpec(
                (rows_per, width),
                lambda i, core, places: (
                    jnp.maximum(i - own_blocks, 0) if len(pieces) == 2 else 0,
                    0,
                ),
            ),
            whole((1, width)),
        ],
        [row, row, pl.BlockSpec((width, rows_per), lambda i, core, places: (0, at(i, core)))],
        [like((length, width)), like((length, width)), like((width, length))],
        prefetch=2,
    )(core, places, own, other, scale)


def turn_body(places, values, out, *, piece):
    put_transposed(out, places, values[...], slice(None), piece)


def turn(places, values, piece, rows_per=256):
    length, width = values.shape
    return call(
        functools.partial(turn_body, piece=piece),
        "turn",
        (length // rows_per,),
        [pl.BlockSpec((rows_per, width), lambda i, places: (i, 0))],
        [pl.BlockSpec((width, rows_per), lambda i, places: (0, i))],
        [like((width, length))],
        prefetch=1,
    )(places, values)[0]


def middle_body(places, *refs, parts, piece):
    mixed = refs[: 2 * parts]
    x, scale, gain, bias, attn, m, mt = refs[2 * parts :]
    total = dot(mixed[0][...], mixed[1][...])
    for part in range(1, parts):
        total += dot(mixed[2 * part][...], mixed[2 * part + 1][...])
    low = total.astype(bf16)
    attn[...] = low
    middle = x[...].astype(f32) + scale[...] * low.astype(f32)
    unit, _ = normalise(middle)
    normed = (unit * gain[...] + bias[...]).astype(bf16)
    m[...] = normed
    put_transposed(mt, places, normed, slice(None), piece)


def middle(places, mixed, x, offset, scale, gain, bias, piece, rows_per=256):
    rows, width = mixed[0][0].shape[0], x.shape[1]
    blocks = rows // rows_per
    specs, operands = [], []
    for left, right in mixed:
        specs += [
            pl.BlockSpec((rows_per, left.shape[1]), lambda i, places: (i, 0)),
            whole(right.shape),
        ]
        operands += [left, right]
    row = pl.BlockSpec((rows_per, width), lambda i, places: (i, 0))
    return call(
        functools.partial(middle_body, parts=len(mixed), piece=piece),
        "middle",
        (blocks,),
        specs
        + [
            pl.BlockSpec((rows_per, width), lambda i, places: (i + offset // rows_per, 0)),
            whole((1, width)),
            whole((1, width)),
            whole((1, width)),
        ],
        [row, row, pl.BlockSpec((width, rows_per), lambda i, places: (0, i))],
        [like((rows, width)), like((rows, width)), like((width, rows))],
        prefetch=1,
    )(places, *operands, x, scale, gain, bias)


def sent_shapes(fast, rows, first, second):
    if fast:
        half = rows // 2
        return [(half, first), (half, first), (half, second), (half, second)]
    return [(rows, first + second)]


def put_rows(outs, fast, quarter, height, left, right):
    if not fast:
        at = slice(quarter * height, quarter * height + height)
        outs[0][at, :] = jnp.concatenate([left, right], axis=1)
        return
    send_a, keep_a, send_b, keep_b = outs
    place = slice((quarter % 2) * height, (quarter % 2) * height + height)
    (send_a if quarter < 2 else keep_a)[place, :] = left
    place = slice((quarter // 2) * height, (quarter // 2) * height + height)
    (send_b if quarter % 2 == 0 else keep_b)[place, :] = right


def feed_body(ma, mb, gm, mta, mtb, gmt, wg, wu, wd, hid, gg, gu, *outs, fast, rows_per):
    half = ma.shape[0]
    for source, base in ((ma, 0), (mb, half)):
        for at in range(0, half, rows_per):
            here = slice(at, at + rows_per)
            there = slice(base + at, base + at + rows_per)
            rows = source[here, :]
            gate = dot(rows, wg[...])
            up = dot(rows, wu[...])
            back = dot(gm[there, :], wd[...], NT)
            sigma = 1.0 / (1.0 + jnp.exp(-gate))
            active = gate * sigma
            hid[there, :] = (active * up).astype(bf16)
            gg[there, :] = (back * up * sigma * (1.0 + gate * (1.0 - sigma))).astype(bf16)
            gu[there, :] = (back * active).astype(bf16)
    width = gmt.shape[0]
    height = width // 4
    columns = hid.shape[1]
    for quarter in range(4):
        rows = slice(quarter * height, quarter * height + height)
        down = dot(gmt[rows, :], hid[...]).astype(bf16)
        left, right = mta[rows, :], mtb[rows, :]
        gate = (dot(left, gg[:half, :]) + dot(right, gg[half:, :])).astype(bf16)
        up = (dot(left, gu[:half, :]) + dot(right, gu[half:, :])).astype(bf16)
        put_rows(
            outs,
            fast,
            quarter,
            height,
            jnp.concatenate([down, gate[:, : columns // 2]], axis=1),
            jnp.concatenate([gate[:, columns // 2 :], up], axis=1),
        )


def feed(fast, m, gm, mt, gmt, wg, wu, wd, first, count, columns, rows_per=256):
    length, width = gm.shape
    half = m[0].shape[0]
    col = pl.BlockSpec((width, columns), lambda j: (0, j + first))
    out = pl.BlockSpec((length, columns), lambda j: (0, j))
    part = columns + columns // 2
    shapes = sent_shapes(fast, width, part, part)
    return call(
        functools.partial(feed_body, fast=fast, rows_per=min(rows_per, half)),
        "feed",
        (count,),
        [whole((half, width))] * 2
        + [whole((length, width))]
        + [whole((width, half))] * 2
        + [whole((width, length))]
        + [col, col, pl.BlockSpec((columns, width), lambda j: (j + first, 0))],
        [out] * 3 + [pl.BlockSpec(shape, lambda j: (0, j)) for shape in shapes],
        [like((length, columns * count))] * 3
        + [like((shape[0], shape[1] * count)) for shape in shapes],
        mib=52,
    )(*m, gm, *mt, gmt, wg, wu, wd)


def split_rows(fast, core, rows, rows_per):
    blocks = rows // rows_per
    own = blocks // 2 if fast else blocks

    def at(i, core):
        return lax.rem(i + (1 - core[0]) * own, blocks) if fast else i

    return blocks, own, at


def multiply_body(core, *refs, parts, dims, own, fast):
    lefts, rights = refs[:parts], refs[parts : 2 * parts]
    total = dot(lefts[0][...], rights[0][...], dims)
    for part in range(1, parts):
        total += dot(lefts[part][...], rights[part][...], dims)
    if fast:
        sent, kept = refs[2 * parts :]

        @pl.when(pl.program_id(0) < own)
        def _():
            sent[...] = total.astype(bf16)

        @pl.when(pl.program_id(0) >= own)
        def _():
            kept[...] = total.astype(bf16)
    else:
        refs[2 * parts][...] = total


def multiply(fast, core, lefts, rights, dims, name, rows_per=256):
    rows = lefts[0].shape[0]
    width = rights[0].shape[1 if dims is NN else 0]
    blocks, own, at = split_rows(fast, core, rows, rows_per)
    left_specs = [
        pl.BlockSpec((rows_per, left.shape[1]), lambda i, core: (at(i, core), 0)) for left in lefts
    ]
    if fast:
        out_specs = [
            pl.BlockSpec((rows_per, width), lambda i, core: (jnp.minimum(i, own - 1), 0)),
            pl.BlockSpec((rows_per, width), lambda i, core: (jnp.maximum(i - own, 0), 0)),
        ]
        out_shape = [like((own * rows_per, width))] * 2
    else:
        out_specs = [pl.BlockSpec((rows_per, width), lambda i, core: (i, 0))]
        out_shape = [like((rows, width), f32)]
    return call(
        functools.partial(multiply_body, parts=len(lefts), dims=dims, own=own, fast=fast),
        name,
        (blocks,),
        left_specs + [whole(right.shape) for right in rights],
        out_specs,
        out_shape,
        prefetch=1,
    )(core, *lefts, *rights)


def middle_back_body(
    core, places, *refs, parts, own_blocks, blocks, piece
):
    partial = refs[:parts]
    x, attn, dy, scale, gain, wo, gh, ga_t, go, sums = refs[parts:]
    step = pl.program_id(0)
    incoming = partial[0][...].astype(f32)
    for part in range(1, parts):
        incoming += partial[part][...].astype(f32)
    attn_rows = attn[...].astype(f32)
    unit, inverse = normalise(x[...].astype(f32) + scale[...] * attn_rows)
    grad = dy[...].astype(f32) + norm_back(incoming, unit, inverse, gain[...])
    gh[...] = grad
    ga = (scale[...] * grad).astype(bf16)
    put_transposed(ga_t, places, ga, slice(None), piece)
    go[...] = dot(ga, wo[...], NT).astype(bf16)

    @pl.when(step == 0)
    def _():
        sums[...] = jnp.zeros_like(sums)

    first = core[0] * own_blocks

    @pl.when((step >= first) & (step < first + own_blocks))
    def _():
        sums[0:1, :] += jnp.sum(incoming * unit, axis=0, keepdims=True)
        sums[1:2, :] += jnp.sum(incoming, axis=0, keepdims=True)
        sums[2:3, :] += jnp.sum(attn_rows * grad, axis=0, keepdims=True)


def middle_back(core, places, partial, x, attn, dy, scale, gain, wo, own_rows, piece, rows_per=256):
    length, width = x.shape
    row = pl.BlockSpec((rows_per, width), lambda i, core, places: (i, 0))
    heads = wo.shape[0]
    half = attn[0].shape[0] // rows_per
    return call(
        functools.partial(
            middle_back_body,
            parts=len(partial),
            own_blocks=own_rows // rows_per if own_rows >= rows_per else 1,
            blocks=length // rows_per,
            piece=piece,
        ),
        "middle_back",
        (length // rows_per,),
        [row] * len(partial) + [row, row, row, whole((1, width)), whole((1, width)), whole(wo.shape)],
        [
            row,
            pl.BlockSpec((width, rows_per), lambda i, core, places: (0, i)),
            pl.BlockSpec((rows_per, heads), lambda i, core, places: (i, 0)),
            whole((8, width)),
        ],
        [
            like((length, width), f32),
            like((width, length)),
            like((length, heads)),
            like((8, width), f32),
        ],
        prefetch=2,
    )(core, places, *partial, x, jnp.concatenate(attn, axis=0), dy, scale, gain, wo)


def weights_body(ut, gat, o, gq, gk, gv, *outs, fast):
    width = ut.shape[0]
    height = width // 4
    for quarter in range(4):
        rows = slice(quarter * height, quarter * height + height)
        left = ut[rows, :]
        put_rows(
            outs,
            fast,
            quarter,
            height,
            jnp.concatenate(
                [dot(left, gq[...]).astype(bf16), dot(gat[rows, :], o[...]).astype(bf16)], axis=1
            ),
            jnp.concatenate(
                [dot(left, gk[...]).astype(bf16), dot(left, gv[...]).astype(bf16)], axis=1
            ),
        )


def attention_weights(fast, ut, gat, o, gq, gk, gv):
    width = ut.shape[0]
    heads = gq.shape[1]
    shapes = sent_shapes(fast, width, 2 * heads, 2 * heads)
    operands = (ut, gat, o, gq, gk, gv)
    return call(
        functools.partial(weights_body, fast=fast),
        "attention_weights",
        (1,),
        [whole(operand.shape) for operand in operands],
        [whole(shape) for shape in shapes],
        [like(shape) for shape in shapes],
    )(*operands)


def output_body(*refs, parts):
    partial = refs[:parts]
    x, attn, dy, scale_attn, scale_mlp, out, sums = refs[parts:]
    total = partial[0][...].astype(f32)
    for part in range(1, parts):
        total += partial[part][...].astype(f32)
    middle_rows = x[...].astype(f32) + scale_attn[...] * attn[...].astype(f32)
    out[...] = (middle_rows + scale_mlp[...] * total).astype(bf16)

    @pl.when(pl.program_id(0) == 0)
    def _():
        sums[...] = jnp.zeros_like(sums)

    sums[3:4, :] += jnp.sum(total * dy[...].astype(f32), axis=0, keepdims=True)


def output_rows(core, partial, x, attn, dy, scale_attn, scale_mlp, rows_per=256):
    rows, width = x.shape
    rows_per = min(rows_per, rows)
    row = pl.BlockSpec((rows_per, width), lambda i: (i, 0))
    return call(
        functools.partial(output_body, parts=len(partial)),
        "output_rows",
        (rows // rows_per,),
        [row] * len(partial) + [row] * 3 + [whole((1, width))] * 2,
        [row, whole((8, width))],
        [like((rows, width)), like((8, width), f32)],
    )(*partial, x, attn, dy, scale_attn, scale_mlp)


def input_body(*refs, parts):
    partial = refs[:parts]
    x, gh, gain, out, sums = refs[parts:]
    incoming = partial[0][...].astype(f32)
    for part in range(1, parts):
        incoming += partial[part][...].astype(f32)
    unit, inverse = normalise(x[...].astype(f32))
    out[...] = (gh[...] + norm_back(incoming, unit, inverse, gain[...])).astype(bf16)

    @pl.when(pl.program_id(0) == 0)
    def _():
        sums[...] = jnp.zeros_like(sums)

    sums[4:5, :] += jnp.sum(incoming * unit, axis=0, keepdims=True)
    sums[5:6, :] += jnp.sum(incoming, axis=0, keepdims=True)


def input_rows(partial, x, gh, gain, rows_per=256):
    rows, width = x.shape
    rows_per = min(rows_per, rows)
    row = pl.BlockSpec((rows_per, width), lambda i: (i, 0))
    return call(
        functools.partial(input_body, parts=len(partial)),
        "input_rows",
        (rows // rows_per,),
        [row] * len(partial) + [row] * 2 + [whole((1, width))],
        [row, whole((8, width))],
        [like((rows, width)), like((8, width), f32)],
    )(*partial, x, gh, gain)


class Wide:
    def __init__(self):
        self.size = lax.axis_size("wide")
        self.fast = self.size == 16
        self.place = lax.axis_index("wide")

    def order(self):
        groups = jnp.arange(self.size, dtype=jnp.int32)
        if not self.fast:
            return groups
        mine = self.place.astype(jnp.int32)
        near = 1 - ((groups ^ mine) & 1)
        far = 1 - (((groups ^ mine) >> 1) & 1)
        line = (groups // 4 - mine // 4) % 4
        return near * 8 + far * 4 + line

    def along(self, values, bit):
        return lax.ppermute(values, "wide", [(i, i ^ bit) for i in range(self.size)])

    def reduce(self, outs):
        if not self.fast:
            return lax.psum_scatter(outs[0], "wide", scatter_dimension=0, tiled=True).astype(f32)
        send_a, keep_a, send_b, keep_b = outs
        part_a = keep_a + self.along(send_a, 1)
        part_b = keep_b + self.along(send_b, 2)
        half = part_a.shape[0] // 2
        part_a = part_a[half:] + self.along(part_a[:half], 2)
        part_b = part_b[half:] + self.along(part_b[:half], 1)
        both = jnp.concatenate([part_a, part_b], axis=1)
        height = both.shape[0] // 4
        total = both[:height].astype(f32)
        for shift in (1, 2, 3):
            moved = lax.ppermute(
                both[shift * height : shift * height + height],
                "wide",
                [(i, (i + 4 * shift) % 16) for i in range(16)],
            )
            total += moved.astype(f32)
        return total


def on_device(
    frames,
    segment_ids,
    w_query,
    w_key,
    w_value,
    w_out,
    w_gate,
    w_up,
    w_down,
    norm1_gain,
    norm1_bias,
    norm2_gain,
    norm2_bias,
    scale_attn,
    scale_mlp,
    output_grad,
):
    paired = lax.axis_size("narrow") == 2
    narrow = lax.axis_index("narrow").astype(jnp.int32)
    core = (narrow if paired else jnp.zeros_like(narrow)).reshape(1)
    wide = Wide()
    places = wide.order()
    rows_own, width = frames.shape
    length = segment_ids.shape[1]
    piece = width // wide.size
    heads = w_query.shape[1]
    units = w_gate.shape[1]
    row = lambda vector: vector.reshape(1, -1)
    gain1, bias1, gain2, bias2 = map(row, (norm1_gain, norm1_bias, norm2_gain, norm2_bias))
    scale1, scale2 = row(scale_attn), row(scale_mlp)

    def swapped(values):
        return lax.ppermute(values, "narrow", [(0, 1), (1, 0)])

    def rows_of_all(values):
        if paired:
            return (values, swapped(values))
        return (lax.all_gather(values, "narrow", axis=0, tiled=True),)

    def own_of(values):
        return lax.dynamic_slice_in_dim(values, narrow * rows_own, rows_own, 0)

    frame_rows = rows_of_all(frames)
    grad_rows = rows_of_all(output_grad)
    q, k, v, u, x, cos, sin = project(
        core, frame_rows, segment_ids, gain1, bias1, w_query, w_key, w_value
    )
    rows_per = 128
    span = rows_per + 2 * HALF_WINDOW
    segw = windows(segment_ids, span)
    half = length // 2
    if paired:
        w_out_all = (w_out, swapped(w_out))
    else:
        w_out_all = (lax.all_gather(w_out, "narrow", axis=0, tiled=True),)
    dy, gm, gmt = cotangent(core, places, grad_rows, scale2, piece)
    mixed, chances, attn, m, mt = [], [], [], [], []
    for part in range(2):
        o_part, p_part = attend(
            q, k, v, segment_ids, segw, part * half // rows_per, half // rows_per, rows_per, span
        )
        mixed.append(o_part)
        chances.append(p_part)
        if paired:
            o_all = (o_part, swapped(o_part))
        else:
            o_all = (lax.all_gather(o_part, "narrow", axis=1, tiled=True),)
        attn_part, m_part, mt_part = middle(
            places, list(zip(o_all, w_out_all)), x, part * half, scale1, gain2, bias2, piece
        )
        attn.append(attn_part)
        m.append(m_part)
        mt.append(mt_part)
    o = jnp.concatenate(mixed, axis=0)

    columns = min(256, units)
    total = units // columns
    counts = [1, 2, 2, 3] if total == 8 else [total]
    hidden, g_gate, g_up, groups = [], [], [], []
    first = 0
    for count in counts:
        hid, gg, gu, *outs = feed(
            wide.fast, m, gm, mt, gmt, w_gate, w_up, w_down, first, count, columns
        )
        hidden.append(hid)
        g_gate.append(gg)
        g_up.append(gu)
        total_rows = wide.reduce(outs)
        if wide.fast:
            total_rows = total_rows.reshape(piece, 2, count, -1).swapaxes(1, 2)
        groups.append(total_rows.reshape(piece, count, 3, columns))
        first += count
    hidden = jnp.concatenate(hidden, axis=1)
    g_gate = jnp.concatenate(g_gate, axis=1)
    g_up = jnp.concatenate(g_up, axis=1)

    def combined(lefts, rights, dims, name, every):
        if paired:
            sent, kept = multiply(True, core, lefts, rights, dims, name)
            return sent, kept
        return multiply(False, core, lefts, rights, dims, name)[0]

    if paired:
        sent, kept = multiply(True, core, [hidden], [w_down], NN, "mlp_out")
        mlp_partial = [kept, swapped(sent)]
        sent, kept = multiply(True, core, [g_gate, g_up], [w_gate, w_up], NT, "norm2_grad")
        both = jnp.concatenate(
            [jnp.where(core[0] == 0, kept, sent), jnp.where(core[0] == 0, sent, kept)], axis=0
        )
        norm2_partial = [both, swapped(both)]
    else:
        part = multiply(False, core, [hidden], [w_down], NN, "mlp_out")[0]
        mlp_partial = [lax.psum_scatter(part, "narrow", scatter_dimension=0, tiled=True)]
        part = multiply(False, core, [g_gate, g_up], [w_gate, w_up], NT, "norm2_grad")[0]
        norm2_partial = [lax.psum(part, "narrow")]
    attn_own = own_of(jnp.concatenate(attn, axis=0))
    output, sums_out = output_rows(
        core, mlp_partial, frames, attn_own, output_grad, scale1, scale2
    )

    gh, gat, go, sums_middle = middle_back(
        core if paired else narrow.reshape(1) * 0,
        places,
        norm2_partial,
        x,
        attn,
        dy,
        scale1,
        gain2,
        w_out,
        rows_own if paired else length,
        piece,
    )
    if not paired:
        sums_middle = jnp.where(narrow == 0, sums_middle, 0.0)
    gq, gk, gv = attend_back(go, q, k, v, chances[0], chances[1], cos, sin, rows_per, span)
    ut = turn(places, u, piece)
    attention = wide.reduce(attention_weights(wide.fast, ut, gat, o, gq, gk, gv))
    attention = attention.reshape(piece, 4, heads)
    if paired:
        sent, kept = multiply(True, core, [gq, gk, gv], [w_query, w_key, w_value], NT, "norm1_grad")
        norm1_partial = [kept, swapped(sent)]
    else:
        part = multiply(False, core, [gq, gk, gv], [w_query, w_key, w_value], NT, "norm1_grad")[0]
        norm1_partial = [lax.psum_scatter(part, "narrow", scatter_dimension=0, tiled=True)]
    input_grad, sums_in = input_rows(norm1_partial, frames, own_of(gh), gain1)
    sums = lax.psum(sums_out + sums_middle + sums_in, ("wide", "narrow"))

    def gathered(at):
        return jnp.concatenate(
            [group[:, :, at].reshape(piece, -1) for group in groups], axis=1
        )

    return (
        output,
        input_grad,
        attention[:, 0],
        attention[:, 2],
        attention[:, 3],
        attention[:, 1].T,
        gathered(1),
        gathered(2),
        gathered(0).T,
        sums[4],
        sums[5],
        sums[0],
        sums[1],
        sums[2],
        sums[3],
    )


def solution(mesh):
    rows = P(("wide", "narrow"), None)
    across = P(None, "narrow")
    return jax.shard_map(
        on_device,
        mesh=mesh,
        in_specs=(rows, P("wide", None))
        + (across,) * 3
        + (P("narrow", None),)
        + (across,) * 2
        + (P("narrow", None),)
        + (P(),) * 6
        + (rows,),
        out_specs=(rows, rows)
        + (P("wide", "narrow"),) * 3
        + (P("narrow", "wide"),)
        + (P("wide", "narrow"),) * 2
        + (P("narrow", "wide"),)
        + (P(),) * 6,
        check_vma=False,
    )
```

```python
import functools
import math

import jax
import jax.numpy as jnp
import numpy as np
from jax import lax
from jax.experimental import pallas as pl
from jax.experimental.pallas import tpu as pltpu
from jax.sharding import PartitionSpec as P

HEAD_DIM = 64
HALF_WINDOW = 64
CLIPS = 6
MAX_CLIP = 384
norm_eps = 1e-05
masked_score = -1e30
COUNTS = [3, 3, 2]
KINDS = ["zy", "zx", "xyz", "xyz", "xyz"]
PLAN = [
    "F0:8", "F1:20", "F2:6", "h0", "mb:3", "a0:3", "turn", "p", "a1:3", "h2", "h1", "ob", "ut",
    "w", "h0", "qa", "hp:3", "h2:3", "oa:1", "qb", "h1:2", "in", "h2:2", "ht", "h0:3", "h1:3",
    "out", "ht", "sum", "hp", "e0", "e1", "s0:3", "ht:10", "hp", "s1:1", "e2:1", "s2:1", "et:10",
    "s3", "ep:6",
]
SHORT = ["F0", "ut", "mb", "p", "a0", "w", "h0", "hp", "ht", "q", "o", "h0", "hp", "ht", "in", "out", "sum", "s0", "s1", "s2", "s3", "h0", "hp", "ht"]
bf16 = jnp.bfloat16
f32 = jnp.float32
NN = (((1,), (0,)), ((), ()))
NT = (((1,), (1,)), ((), ()))
TN = (((0,), (0,)), ((), ()))


def dot(a, b, dims=NN):
    return lax.dot_general(a, b, dims, preferred_element_type=f32)


class Chain:
    token = None
    held = []
    weight = 0


def call(
    body,
    name,
    grid,
    in_specs,
    out_specs,
    out_shape,
    scratch=(),
    prefetch=0,
    mib=16,
    aliases=None,
    near_in=(),
    near_out=(),
):
    outputs = len(out_specs)
    before = [] if Chain.token is None else [(Chain.token, pltpu.HBM)]
    before += [(one, pltpu.VMEM) for one in Chain.held]
    Chain.held = []
    extra = len(before)
    weight, Chain.weight = 1 + Chain.weight, 0

    def inner(*refs):
        rest = refs[prefetch + extra :]
        ins = len(in_specs)
        body(*refs[:prefetch], *rest[: ins + outputs], *rest[ins + outputs + 1 :])

    anywhere = pl.BlockSpec(memory_space=pl.ANY)
    shapes = [
        (pltpu.VMEM if at in near_out else pltpu.HBM)(one.shape, one.dtype)
        for at, one in enumerate(out_shape)
    ]
    run = pl.pallas_call(
        inner,
        grid_spec=pltpu.PrefetchScalarGridSpec(
            num_scalar_prefetch=prefetch,
            grid=grid,
            in_specs=[anywhere] * extra + list(in_specs),
            out_specs=list(out_specs) + [anywhere],
            scratch_shapes=list(scratch),
        ),
        out_shape=shapes + [pltpu.HBM((8, 128), f32)],
        input_output_aliases={at + extra: out for at, out in (aliases or {}).items()},
        compiler_params=pltpu.CompilerParams(vmem_limit_bytes=mib * 2**20),
        cost_estimate=pl.CostEstimate(flops=weight, bytes_accessed=1, transcendentals=0),
        name=name,
    )

    def apply(*operands):
        placed = before + [
            (one, pltpu.VMEM if at in near_in else pltpu.HBM)
            for at, one in enumerate(operands[prefetch:])
        ]
        placed = [pltpu.with_memory_space_constraint(*one) for one in placed]
        *results, Chain.token = run(*operands[:prefetch], *placed)
        return results

    return apply


def near(shape):
    return pl.BlockSpec(memory_space=pltpu.VMEM)


def whole(shape):
    return pl.BlockSpec(
        shape, lambda *_: (0,) * len(shape), pipeline_mode=pl.Buffered(1)
    )


def like(shape, kind=bf16):
    return jax.ShapeDtypeStruct(shape, kind)


def normalise(rows):
    centred = rows - jnp.mean(rows, axis=-1, keepdims=True)
    inverse = lax.rsqrt(jnp.mean(centred * centred, axis=-1, keepdims=True) + norm_eps)
    return centred * inverse, inverse


def norm_back(incoming, unit, inverse, gain):
    scaled = incoming * gain
    return inverse * (
        scaled
        - jnp.mean(scaled, axis=-1, keepdims=True)
        - unit * jnp.mean(scaled * unit, axis=-1, keepdims=True)
    )


def rope_table():
    half = HEAD_DIM // 2
    lane = np.arange(128)
    frequency = np.exp((lane % half) * (-math.log(10000.0) / half))
    angle = np.arange(MAX_CLIP)[:, None] * frequency[None, :]
    sign = np.where(lane % HEAD_DIM < half, -1.0, 1.0)
    parts = []
    for table in (np.cos(angle), np.sin(angle) * sign):
        high = table.astype(np.float32).astype(bf16)
        parts += [high, (table - high.astype(np.float64)).astype(np.float32).astype(bf16)]
    return np.concatenate(parts, axis=1)


def swap_halves(values):
    half = HEAD_DIM // 2
    width = values.shape[-1]
    lane = lax.broadcasted_iota(jnp.int32, values.shape, 1)
    return jnp.where(
        lane % HEAD_DIM < half,
        pltpu.roll(values, width - half, 1),
        pltpu.roll(values, half, 1),
    )


def column_of(row, start, count):
    pieces = []
    for place in range(count // 128):
        piece = row[:, pl.ds(pl.multiple_of(start + place * 128, 128), 128)]
        pieces.append(jnp.broadcast_to(piece.astype(f32), (128, 128)).T)
    return jnp.concatenate(pieces, axis=0) if len(pieces) > 1 else pieces[0]


def project_body(base, *refs, parts):
    xs = refs[:parts]
    seg, gain, bias, table, wq, wk, wv, q, k, v, cos, sin, clips, kept = refs[parts:]
    step, blocks = pl.program_id(0), pl.num_programs(0)
    block = lax.rem(base[0] + step, blocks)
    rows_per = xs[0].shape[0]
    raw = xs[0][...]
    for part in range(1, parts):
        raw = jnp.where(step >= part * (blocks // parts), xs[part][...], raw)
    unit, _ = normalise(raw.astype(f32))
    normed = (unit * gain[...] + bias[...]).astype(bf16)
    kept[...] = normed
    ids = seg[...]
    mine = column_of(seg, block * rows_per, rows_per)
    clips[...] = mine
    start = jnp.zeros_like(mine)
    for clip in range(CLIPS - 1):
        count = jnp.sum((ids == clip).astype(f32), axis=-1, keepdims=True)
        start += jnp.where(mine > clip, count, 0.0)
    place = lax.broadcasted_iota(jnp.int32, mine.shape, 0) + block * rows_per
    place = place - start.astype(jnp.int32)
    lane = lax.broadcasted_iota(jnp.int32, mine.shape, 1)
    hot = jnp.concatenate(
        [(place == lane + 128 * part).astype(bf16) for part in range(MAX_CLIP // 128)], axis=1
    )
    rows = dot(hot, table[...])
    cosine = rows[:, :128] + rows[:, 128:256]
    sine = rows[:, 256:384] + rows[:, 384:]
    cos[...] = cosine
    sin[...] = sine
    for weights, out, factor in ((wq, q, HEAD_DIM**-0.5), (wk, k, 1.0)):
        flat = dot(normed, weights[...])
        for at in range(0, flat.shape[1], 128):
            part = flat[:, at : at + 128]
            part = part * cosine + swap_halves(part) * sine
            out[:, at : at + 128] = (part * factor).astype(bf16)
    v[...] = dot(normed, wv[...]).astype(bf16)


def project(base, xs, seg, gain, bias, wq, wk, wv, rows_per=256):
    parts = len(xs)
    each, width = xs[0].shape
    length = parts * each
    heads = wq.shape[1]
    blocks = length // rows_per

    def out(columns):
        return pl.BlockSpec((rows_per, columns), lambda i, base: (lax.rem(base[0] + i, blocks), 0))

    def piece(part):
        count = each // rows_per
        return pl.BlockSpec(
            (rows_per, width), lambda i, base: (jnp.clip(i - part * count, 0, count - 1), 0)
        )

    table = rope_table()
    return call(
        functools.partial(project_body, parts=parts),
        "project",
        (blocks,),
        [piece(part) for part in range(parts)]
        + [
            whole(seg.shape),
            whole((1, width)),
            whole((1, width)),
            whole(table.shape),
            whole(wq.shape),
            whole(wk.shape),
            whole(wv.shape),
        ],
        [out(heads)] * 3
        + [out(128)] * 3
        + [pl.BlockSpec((rows_per, width), lambda i, base: (i, 0))],
        [like((length, heads))] * 3 + [like((length, 128), f32)] * 3 + [like((length, width))],
        prefetch=1,
        near_in=range(1, parts),
        near_out=[0, 1, 2, 5],
    )(base, *xs, seg, gain, bias, jnp.asarray(table), wq, wk, wv)


def band(block, rows_per, span, length):
    first = block * rows_per
    start = jnp.clip(first - HALF_WINDOW, 0, length - span)
    return first, pl.multiple_of(start, HALF_WINDOW)


def two_heads(values):
    lane = lax.broadcasted_iota(jnp.int32, values.shape, 1)
    zero = jnp.zeros_like(values)
    return jnp.concatenate(
        [jnp.where(lane < HEAD_DIM, values, zero), jnp.where(lane < HEAD_DIM, zero, values)], axis=0
    )


def one_each(stacked):
    count = stacked.shape[0] // 2
    lane = lax.broadcasted_iota(jnp.int32, (count, 128), 1)
    return jnp.where(lane < HEAD_DIM, stacked[:count], stacked[count:])


def attend_body(base, q, k, v, seg, clips, *refs, span):
    o, weights = refs[-2:]
    rows_per = q.shape[0]
    length = k.shape[0]
    block = base[0] + pl.program_id(0)
    first, start = band(block, rows_per, span, length)
    mine = seg[:, pl.ds(first, rows_per)]
    theirs = clips[pl.ds(start, span), :]
    gap = (
        lax.broadcasted_iota(jnp.int32, (span, rows_per), 0)
        - lax.broadcasted_iota(jnp.int32, (span, rows_per), 1)
        + (start - first)
    )
    allowed = (gap >= -HALF_WINDOW) & (gap < HALF_WINDOW) & (theirs == mine.astype(f32))
    penalty = jnp.where(allowed, 0.0, masked_score)
    penalty = jnp.concatenate([penalty, penalty], axis=1)
    for pair in range(q.shape[1] // 128):
        lanes = slice(pair * 128, pair * 128 + 128)
        keys = k[pl.ds(start, span), lanes]
        values = v[pl.ds(start, span), lanes]
        scores = dot(keys, two_heads(q[:, lanes]), NT) + penalty
        lifted = jnp.exp(scores - jnp.max(scores, axis=0, keepdims=True))
        chances = (lifted * (1.0 / jnp.sum(lifted, axis=0, keepdims=True))).astype(bf16)
        weights[0, pair] = chances
        o[:, lanes] = one_each(dot(chances, values, TN)).astype(bf16)


def attend(base, q, k, v, seg, clips, blocks, rows_per, span, weights=None):
    length, heads = q.shape
    pairs = heads // 128
    kept = [] if weights is None else [weights]
    return call(
        functools.partial(attend_body, span=span),
        "attend",
        (blocks,),
        [
            pl.BlockSpec((rows_per, heads), lambda i, base: (base[0] + i, 0)),
            near(k.shape),
            near(v.shape),
            whole(seg.shape),
            near(clips.shape),
        ]
        + [pl.BlockSpec(memory_space=pl.ANY)] * len(kept),
        [
            pl.BlockSpec((rows_per, heads), lambda i, base: (i, 0)),
            pl.BlockSpec((1, pairs, span, 2 * rows_per), lambda i, base: (base[0] + i, 0, 0, 0)),
        ],
        [like((blocks * rows_per, heads)), like((length // rows_per, pairs, span, 2 * rows_per))],
        prefetch=1,
        aliases={6: 1} if kept else None,
        near_in=[0, 1, 2, 4],
    )(base, q, k, v, seg, clips, *kept)


def attend_back_body(base, *refs, parts, span, start, last):
    ga, wo, q, k, v, weights, cos, sin, *refs = refs[:parts], *refs[parts:]
    gq, gk, gv, acc_k, acc_v = refs[-5:]
    rows_per = q.shape[0]
    length = k.shape[0]
    block = base[0] + pl.program_id(0)
    _, first = band(block, rows_per, span, length)

    if start:

        @pl.when(pl.program_id(0) == 0)
        def _():
            acc_k[...] = jnp.zeros_like(acc_k)
            acc_v[...] = jnp.zeros_like(acc_v)

    rows = ga[0][...]
    for part in range(1, parts):
        rows = jnp.where(pl.program_id(0) >= part * (pl.num_programs(0) // parts), ga[part][...], rows)
    go = dot(rows, wo[...], NT).astype(bf16)
    mine = pl.ds(pl.multiple_of(block * rows_per, rows_per), rows_per)
    cosine, sine = cos[mine, :], sin[mine, :]
    keys_at = pl.ds(first, span)
    for pair in range(q.shape[1] // 128):
        lanes = slice(pair * 128, pair * 128 + 128)
        keys = k[keys_at, lanes]
        values = v[keys_at, lanes]
        chances = weights[0, pair]
        full = chances.astype(f32)
        go_two = two_heads(go[:, lanes])
        change = dot(values, go_two, NT)
        weighted = jnp.sum(full * change, axis=0, keepdims=True)
        gs = (full * (change - weighted)).astype(bf16)
        gq_rows = one_each(dot(gs, keys, TN)) * HEAD_DIM**-0.5
        gq[:, lanes] = (gq_rows * cosine - swap_halves(gq_rows) * sine).astype(bf16)
        acc_k[keys_at, lanes] += dot(gs, two_heads(q[:, lanes]))
        acc_v[keys_at, lanes] += dot(chances, go_two)

    if last:

        @pl.when(pl.program_id(0) == pl.num_programs(0) - 1)
        def _():
            @pl.loop(0, length // rows_per)
            def _(at):
                here = pl.ds(pl.multiple_of(at * rows_per, rows_per), rows_per)
                gv[here, :] = acc_v[here, :].astype(bf16)
                for pair in range(q.shape[1] // 128):
                    lanes = slice(pair * 128, pair * 128 + 128)
                    rows = acc_k[here, lanes]
                    rows = rows * cos[here, :] - swap_halves(rows) * sin[here, :]
                    gk[here, lanes] = rows.astype(bf16)


def attend_back(base, ga, wo, q, k, v, weights, cos, sin, rows_per, span, kept, last):
    length, heads = q.shape
    pairs = heads // 128
    parts = len(ga)
    each, width = ga[0].shape
    rows = parts * each
    row = pl.BlockSpec((rows_per, heads), lambda i, base: (base[0] + i, 0))
    full = near((length, heads))

    def block(part):
        count = each // rows_per
        return pl.BlockSpec(
            (rows_per, width), lambda i, base: (jnp.clip(i - part * count, 0, count - 1), 0)
        )

    return call(
        functools.partial(
            attend_back_body, parts=parts, span=span, start=not kept, last=last
        ),
        "attend_back",
        (rows // rows_per,),
        [block(part) for part in range(parts)]
        + [
            whole(wo.shape),
            row,
            full,
            full,
            pl.BlockSpec((1, pairs, span, 2 * rows_per), lambda i, base: (base[0] + i, 0, 0, 0)),
            whole(cos.shape),
            whole(sin.shape),
        ]
        + [full if at > 0 else pl.BlockSpec(memory_space=pl.ANY) for at in range(len(kept))],
        [row, full, full, full, full],
        [like((length, heads))] * 3 + [like((length, heads), f32)] * 2,
        prefetch=1,
        aliases={8 + parts + at: at for at in range(len(kept))},
        near_in=list(range(parts))
        + [parts + at for at in (1, 2, 3)]
        + [parts + 7 + at for at in range(len(kept))],
        near_out=range(5),
    )(base, *ga, wo, q, k, v, weights, cos, sin, *kept)


def put_transposed(target, values):
    for at in range(0, values.shape[1], 128):
        target[at : at + 128, :] = values[:, at : at + 128].T


def cotangent_body(dy, scale, gm, gmt):
    scaled = (dy[...].astype(f32) * scale[...]).astype(bf16)
    gm[...] = scaled
    put_transposed(gmt, scaled)


def cotangent(dy, scale, near_in=0, rows_per=256):
    rows, width = dy.shape
    row = pl.BlockSpec((rows_per, width), lambda i: (i, 0))
    return call(
        cotangent_body,
        "cotangent",
        (rows // rows_per,),
        [row, whole((1, width))],
        [row, pl.BlockSpec((width, rows_per), lambda i: (0, i))],
        [like((rows, width)), like((width, rows))],
        near_in=range(near_in),
        near_out=range(2 * near_in),
    )(dy, scale)


def turn_body(values, out, *copies):
    put_transposed(out, values[...])
    for copy in copies:
        copy[...] = values[...]


def turn(values, near_in=0, near_out=0, start=0, length=None, copies=0, rows_per=256):
    width = values.shape[1]
    length = length or values.shape[0]
    rows_per = min(rows_per, length)
    first = start // rows_per
    results = call(
        turn_body,
        "turn",
        (length // rows_per,),
        [pl.BlockSpec((rows_per, width), lambda i: (i + first, 0))],
        [pl.BlockSpec((width, rows_per), lambda i: (0, i))]
        + [pl.BlockSpec((rows_per, width), lambda i: (i, 0))] * copies,
        [like((width, length))] + [like((length, width))] * copies,
        near_in=range(near_in),
        near_out=list(range(near_out)) + list(range(1, 1 + copies)),
    )(values)
    return results if copies else results[0]


def middle_body(*refs, parts):
    mixed = refs[: 2 * parts]
    x, scale, gain, bias = refs[2 * parts : 2 * parts + 4]
    attn, m, mt, *sent = refs[2 * parts + 4 :]
    total = dot(mixed[0][...], mixed[1][...])
    for part in range(1, parts):
        total += dot(mixed[2 * part][...], mixed[2 * part + 1][...])
    low = total.astype(bf16)
    attn[...] = low
    rows = x[...].astype(f32) + scale[...] * low.astype(f32)
    unit, _ = normalise(rows)
    normed = (unit * gain[...] + bias[...]).astype(bf16)
    m[...] = normed
    put_transposed(mt, normed)
    for copy in sent:
        copy[...] = normed


def middle(mixed, x, scale, gain, bias, sent, rows_per=256):
    rows, width = x.shape
    specs, operands = [], []
    for left, right in mixed:
        specs += [
            pl.BlockSpec((rows_per, left.shape[1]), lambda i: (i, 0)),
            whole(right.shape),
        ]
        operands += [left, right]
    row = pl.BlockSpec((rows_per, width), lambda i: (i, 0))
    return call(
        functools.partial(middle_body, parts=len(mixed)),
        "middle",
        (rows // rows_per,),
        specs + [row, whole((1, width)), whole((1, width)), whole((1, width))],
        [row, row, pl.BlockSpec((width, rows_per), lambda i: (0, i))] + [row] * sent,
        [like((rows, width)), like((rows, width)), like((width, rows))]
        + [like((rows, width))] * sent,
        near_in=[2, 3] * (len(mixed) > 1),
    )(*operands, x, scale, gain, bias)


def gathered(source, back, quarter, piece):
    groups = source.shape[0] // (4 * piece)
    return jnp.concatenate(
        [
            source[pl.ds(pl.multiple_of(back[quarter * groups + at] * piece, piece), piece), :]
            for at in range(groups)
        ],
        axis=0,
    )


def put_quarter(sent, kept, quarter, start, values):
    height = values.shape[0]
    place = slice((quarter % 2) * height, (quarter % 2) * height + height)
    (sent if quarter < 2 else kept)[place, start : start + values.shape[1]] = values


def feed_grads_body(back, *refs, parts):
    mt, gmt = refs[:parts], refs[parts : 2 * parts]
    hid, gg, gu, sent, kept = refs[2 * parts :]
    piece = gmt[0].shape[0] // back.shape[0]
    columns = hid.shape[1]
    each = gmt[0].shape[1]

    def product(lefts, right):
        total = dot(lefts[0], right[:each, :])
        for part in range(1, parts):
            total += dot(lefts[part], right[part * each : part * each + each, :])
        return total.astype(bf16)

    for quarter in range(4):
        grad_rows = [gathered(source, back, quarter, piece) for source in gmt]
        put_quarter(sent, kept, quarter, 0, product(grad_rows, hid))
        rows = [gathered(source, back, quarter, piece) for source in mt]
        put_quarter(sent, kept, quarter, columns, product(rows, gg))
        put_quarter(sent, kept, quarter, 2 * columns, product(rows, gu))


def feed_acts_body(m, gm, wg, wu, wd, hid, gg, gu, total, fresh, rows_per):
    each = m[0].shape[0]
    for part in range(len(m)):

        @pl.loop(0, each // rows_per)
        def _(at, part=part):
            here = pl.ds(pl.multiple_of(at * rows_per, rows_per), rows_per)
            there = pl.ds(pl.multiple_of(part * each + at * rows_per, rows_per), rows_per)
            rows = m[part][here, :]
            gate = dot(rows, wg[...])
            up = dot(rows, wu[...])
            back = dot(gm[part][here, :], wd[...], NT)
            sigma = 1.0 / (1.0 + jnp.exp(-gate))
            active = gate * sigma
            hid[there, :] = (active * up).astype(bf16)
            gate_back = (back * up * sigma * (1.0 + gate * (1.0 - sigma))).astype(bf16)
            up_back = (back * active).astype(bf16)
            gg[there, :] = gate_back
            gu[there, :] = up_back
            both = jnp.concatenate([gate_back, up_back], axis=1)
            for start in range(0, total.shape[1], 256):
                cols = slice(start, start + 256)
                weights = jnp.concatenate([wg[cols, :], wu[cols, :]], axis=1)
                more = dot(both, weights, NT)
                total[there, cols] = jnp.where(fresh, more, total[there, cols] + more)


def feed_body(back, *refs, parts, rows_per, first, sent_blocks):
    m, gm, mt, gmt = (refs[at * parts : (at + 1) * parts] for at in range(4))
    wg, wu, wd, *refs = refs[4 * parts :]
    gg, gu = refs[-2:]
    hid, sent, kept, total, *blocks = refs[-6 - sent_blocks : -2]
    step = pl.program_id(0)
    if first:
        start = step == 0
    else:
        start = step < 0

    feed_acts_body(m, gm, wg, wu, wd, hid, gg, gu, total, start, rows_per)
    feed_grads_body(back, *mt, *gmt, hid, gg, gu, sent, kept, parts=parts)
    if blocks:

        @pl.when(step == pl.num_programs(0) - 1)
        def _():
            height = blocks[0].shape[0]
            base = total.shape[0] // 2
            for at, out in enumerate(blocks):
                out[...] = total[base + at * height : base + at * height + height, :].astype(bf16)


def feed(back, m, gm, mt, gmt, wg, wu, wd, first, count, columns, total, sent_blocks, rows_per=512):
    each, width = gm[0].shape
    parts = len(gm)
    length = each * parts
    col = pl.BlockSpec((width, columns), lambda j, back: (0, j + first))
    out = pl.BlockSpec((length, columns), lambda j, back: (0, j))
    grad = pl.BlockSpec((width // 2, 3 * columns), lambda j, back: (0, j))
    so_far = [] if total is None else [total]
    block = (length // 2 // max(sent_blocks, 1), width)
    return call(
        functools.partial(
            feed_body, parts=parts, rows_per=rows_per, first=total is None, sent_blocks=sent_blocks
        ),
        "feed",
        (count,),
        [near((each, width))] * (4 * parts)
        + [col, col, pl.BlockSpec((columns, width), lambda j, back: (j + first, 0))]
        + [near((length, width))] * len(so_far),
        [out] + [grad] * 2 + [near((length, width))] + [whole(block)] * sent_blocks,
        [like((length, columns * count))]
        + [like((width // 2, 3 * columns * count))] * 2
        + [like((length, width), f32)]
        + [like(block)] * sent_blocks,
        scratch=[pltpu.VMEM((length, columns), bf16)] * 2,
        prefetch=1,
        near_in=list(range(4 * parts)) + [4 * parts + 3] * len(so_far),
        near_out=range(1, 4 + sent_blocks),
        aliases={4 * parts + 4: 3} if so_far else None,
        mib=24,
    )(back, *m, *gm, *mt, *gmt, wg, wu, wd, *so_far)


def multiply_body(base, *refs, counts, dims):
    lefts, rights = refs[: sum(counts)], refs[sum(counts) : sum(counts) + len(counts)]
    outs = refs[sum(counts) + len(counts) :]
    total = None
    piece = 0
    for count, right in zip(counts, rights):
        at = 0
        for left in lefts[piece : piece + count]:
            depth = left.shape[1]
            if dims is NN:
                part = dot(left[...], right[at : at + depth, :])
            else:
                part = dot(left[...], right[:, at : at + depth], NT)
            total = part if total is None else total + part
            at += depth
        piece += count
    total = total.astype(outs[0].dtype)
    if len(outs) == 1:
        outs[0][...] = total
        return
    for block, out in enumerate(outs):

        @pl.when(pl.program_id(0) == block)
        def _(out=out):
            out[...] = total


def multiply(base, rows, lefts, rights, dims, name, kind=bf16, rows_per=256, near_in=(), near_out=(), apart=False):
    width = rights[0].shape[1 if dims is NN else 0]
    pieces = [piece for left in lefts for piece in left]
    return call(
        functools.partial(multiply_body, counts=[len(left) for left in lefts], dims=dims),
        name,
        (rows // rows_per,),
        [
            pl.BlockSpec((rows_per, piece.shape[1]), lambda i, base: (base[0] + i, 0))
            for piece in pieces
        ]
        + [whole(right.shape) for right in rights],
        [whole((rows_per, width))] * (rows // rows_per)
        if apart
        else [pl.BlockSpec((rows_per, width), lambda i, base: (i, 0))],
        [like((rows_per, width), kind)] * (rows // rows_per)
        if apart
        else [like((rows, width), kind)],
        prefetch=1,
        mib=24,
        near_in=near_in,
        near_out=near_out,
    )(base, *pieces, *rights)


def middle_back_body(*refs, parts):
    pieces = sum(parts)
    x, attn, dy, scale, gain, gh, ga, gat, sums, *sent = refs[pieces:]
    step = pl.program_id(0)
    incoming = None
    at = 0
    for count in parts:
        rows = refs[at][...].astype(f32)
        for block in range(1, count):
            rows = jnp.where(step == block, refs[at + block][...].astype(f32), rows)
        incoming = rows if incoming is None else incoming + rows
        at += count
    attn_rows = attn[...].astype(f32)
    unit, inverse = normalise(x[...].astype(f32) + scale[...] * attn_rows)
    grad = dy[...].astype(f32) + norm_back(incoming, unit, inverse, gain[...])
    gh[...] = grad
    low = (scale[...] * grad).astype(bf16)
    ga[...] = low
    for block, out in enumerate(sent):

        @pl.when(step == block)
        def _(out=out):
            out[...] = low

    put_transposed(gat, low)

    @pl.when(step == 0)
    def _():
        sums[...] = jnp.zeros_like(sums)

    sums[0:1, :] += jnp.sum(incoming * unit, axis=0, keepdims=True)
    sums[1:2, :] += jnp.sum(incoming, axis=0, keepdims=True)
    sums[2:3, :] += jnp.sum(attn_rows * grad, axis=0, keepdims=True)


def middle_back(partial, x, attn, dy, scale, gain, sent, rows_per=256):
    rows, width = x.shape
    blocks = rows // rows_per
    row = pl.BlockSpec((rows_per, width), lambda i: (i, 0))
    partial = [part if isinstance(part, list) else [part] for part in partial]
    specs = [
        row if len(part) == 1 else whole((rows_per, width)) for part in partial for _ in part
    ]
    flat = [block for part in partial for block in part]
    return call(
        functools.partial(middle_back_body, parts=[len(part) for part in partial]),
        "middle_back",
        (blocks,),
        specs + [row, row, row, whole((1, width)), whole((1, width))],
        [
            row,
            row,
            pl.BlockSpec((width, rows_per), lambda i: (0, i)),
            whole((8, width)),
        ]
        + [whole((rows_per, width))] * (blocks * sent),
        [
            like((rows, width), f32),
            like((rows, width)),
            like((width, rows)),
            like((8, width), f32),
        ]
        + [like((rows_per, width))] * (blocks * sent),
        near_in=range(len(flat)),
        near_out=[1, 2] + list(range(4, 4 + blocks * sent)),
    )(*flat, x, attn, dy, scale, gain)


def weights_body(core, back, *refs, parts):
    ut, (gq, gk, gv, sent, kept) = refs[:parts], refs[parts:]
    piece = ut[0].shape[0] // back.shape[0]
    each = ut[0].shape[1]
    heads = gq.shape[1]

    def product(lefts, right):
        total = None
        for part in range(parts):
            first = (core[0] if part == 0 else 1 - core[0]) * each if parts == 2 else 0
            there = pl.ds(pl.multiple_of(first, each), each) if parts == 2 else slice(None)
            one = dot(lefts[part], right[there, :])
            total = one if total is None else total + one
        return total.astype(bf16)

    for quarter in range(4):
        rows = [gathered(source, back, quarter, piece) for source in ut]
        for place, right in enumerate((gq, gk, gv)):
            put_quarter(sent, kept, quarter, place * heads, product(rows, right))


def attention_weights(core, back, ut, gq, gk, gv):
    width = ut[0].shape[0]
    shape = (width // 2, 3 * gq.shape[1])
    operands = (*ut, gq, gk, gv)
    parts = len(ut)
    close = [parts + at for at in range(3)]
    return call(
        functools.partial(weights_body, parts=parts),
        "attention_weights",
        (1,),
        [(near if at in close else whole)(one.shape) for at, one in enumerate(operands)],
        [near(shape)] * 2,
        [like(shape)] * 2,
        prefetch=2,
        near_in=close,
        near_out=range(2),
    )(core, back, *operands)


def proj_body(back, *refs, parts, blocks):
    gat, o, (sent, kept) = refs[:blocks], refs[blocks : blocks + parts], refs[blocks + parts :]
    piece = gat[0].shape[0] // back.shape[0]
    each = o[0].shape[0]
    for quarter in range(4):
        proj = None
        at = 0
        for block in gat:
            size = block.shape[1]
            right = o[at // each][at % each : at % each + size, :]
            one = dot(gathered(block, back, quarter, piece), right)
            proj = one if proj is None else proj + one
            at += size
        put_quarter(sent, kept, quarter, 0, proj.astype(bf16))


def proj_weights(back, gat, o):
    shape = (gat[0].shape[0] // 2, o[0].shape[1])
    parts, blocks = len(o), len(gat)
    return call(
        functools.partial(proj_body, parts=parts, blocks=blocks),
        "proj_weights",
        (1,),
        [near(one.shape) for one in gat] + [whole(one.shape) for one in o],
        [near(shape)] * 2,
        [like(shape)] * 2,
        prefetch=1,
        near_in=range(blocks),
        near_out=range(2),
    )(back, *gat, *o)


def output_body(core, *refs, parts):
    partial = refs[:parts]
    x, attn, dy, scale_attn, scale_mlp, out, sums = refs[parts:]
    total = partial[0][...].astype(f32)
    for part in range(1, parts):
        total += partial[part][...].astype(f32)
    middle_rows = x[...].astype(f32) + scale_attn[...] * attn[...].astype(f32)
    out[...] = (middle_rows + scale_mlp[...] * total).astype(bf16)

    @pl.when(pl.program_id(0) == 0)
    def _():
        sums[...] = jnp.zeros_like(sums)

    sums[3:4, :] += jnp.sum(total * dy[...].astype(f32), axis=0, keepdims=True)


def output_rows(core, partial, x, attn, dy, scale_attn, scale_mlp, rows_per=256):
    rows, width = x.shape
    rows_per = min(rows_per, rows)
    row = pl.BlockSpec((rows_per, width), lambda i, core: (i, 0))
    own = pl.BlockSpec((rows_per, width), lambda i, core: (i + core[0], 0))
    return call(
        functools.partial(output_body, parts=len(partial)),
        "output_rows",
        (rows // rows_per,),
        [row] * len(partial) + [row, own, row] + [whole((1, width))] * 2,
        [row, whole((8, width))],
        [like((rows, width)), like((8, width), f32)],
        prefetch=1,
        near_in=range(len(partial)),
    )(core, *partial, x, attn, dy, scale_attn, scale_mlp)


def input_body(core, *refs, parts):
    partial = refs[:parts]
    x, gh, gain, out, sums = refs[parts:]
    incoming = partial[0][...].astype(f32)
    for part in range(1, parts):
        incoming += partial[part][...].astype(f32)
    unit, inverse = normalise(x[...].astype(f32))
    out[...] = (gh[...] + norm_back(incoming, unit, inverse, gain[...])).astype(bf16)

    @pl.when(pl.program_id(0) == 0)
    def _():
        sums[...] = jnp.zeros_like(sums)

    sums[4:5, :] += jnp.sum(incoming * unit, axis=0, keepdims=True)
    sums[5:6, :] += jnp.sum(incoming, axis=0, keepdims=True)


def input_rows(core, partial, x, gh, gain, rows_per=256):
    rows, width = x.shape
    rows_per = min(rows_per, rows)
    row = pl.BlockSpec((rows_per, width), lambda i, core: (i, 0))
    own = pl.BlockSpec((rows_per, width), lambda i, core: (i + core[0], 0))
    return call(
        functools.partial(input_body, parts=len(partial)),
        "input_rows",
        (rows // rows_per,),
        [row] * len(partial) + [row, own] + [whole((1, width))],
        [row, whole((8, width))],
        [like((rows, width)), like((8, width), f32)],
        prefetch=1,
        near_in=range(len(partial)),
    )(core, *partial, x, gh, gain)


class Wide:
    def __init__(self):
        self.size = lax.axis_size("wide")
        self.bits = self.size.bit_length() - 1
        assert self.size == 1 << self.bits and self.bits > 2
        self.place = lax.axis_index("wide").astype(jnp.int32)
        self.cores = lax.axis_size("narrow")
        self.core = lax.axis_index("narrow")

    def orders(self, kind):
        rest = list(range(2, self.bits))
        near_far, far_near = [0, 1] + rest, [1, 0] + rest
        return {
            "xyz": (near_far, far_near),
            "zy": (near_far, rest + [1, 0]),
            "zx": (rest + [0, 1], far_near),
            "mid": ([0] + rest + [1], [1] + rest + [0]),
        }[kind]

    def back(self, kind):
        found = []
        for order in self.orders(kind):
            groups = []
            for place in range(self.size):
                apart = 0
                for step, bit in enumerate(order):
                    apart |= (1 - ((place >> (self.bits - 1 - step)) & 1)) << bit
                groups.append(apart)
            found.append(jnp.array(groups, jnp.int32))
        return self.place ^ jnp.where(self.core % 2 == 0, *found)

    def hop(self, values, kind, step):
        orders = self.orders(kind)
        pairs = []
        for group in range(self.size):
            for core in range(self.cores):
                target = group ^ (1 << orders[core % 2][step])
                pairs.append((group * self.cores + core, target * self.cores + core))
        return lax.ppermute(values, ("wide", "narrow"), pairs)

    def along(self, values, bit):
        return lax.ppermute(values, "wide", [(i, i ^ (1 << bit)) for i in range(self.size)])


class Group:
    def __init__(self, wide, kind, sent, kept):
        self.wide, self.kind, self.step = wide, kind, 0
        self.kept, self.got = kept, wide.hop(sent, kind, 0)

    def advance(self):
        sent, self.kept = add_again(self.kept, self.got)
        self.step += 1
        self.got = self.wide.hop(sent, self.kind, self.step)


def add_body(left, right, out):
    out[...] = left[...] + right[...]


def add(left, right):
    return call(
        add_body,
        "add",
        (),
        [near(left.shape)] * 2,
        [near(left.shape)],
        [like(left.shape, left.dtype)],
        near_in=range(2),
        near_out=range(1),
    )(left, right)[0]


def add_again_body(keep, got, sent, rest):
    half = sent.shape[0]
    sent[...] = keep[:half, :] + got[:half, :]
    rest[...] = keep[half:, :] + got[half:, :]


def add_again(keep, got):
    shape = (keep.shape[0] // 2, keep.shape[1])
    return call(
        add_again_body,
        "add_again",
        (),
        [near(keep.shape)] * 2,
        [near(shape)] * 2,
        [like(shape)] * 2,
        near_in=range(2),
        near_out=range(2),
    )(keep, got)


def finish_feed_body(*refs, counts, columns):
    gate, up, down = refs[-3:]
    at = 0
    for group, count in enumerate(counts):
        kept, got = refs[2 * group : 2 * group + 2]
        for block in range(count):
            for part, out in enumerate((down, gate, up)):
                there = slice((3 * block + part) * columns, (3 * block + part + 1) * columns)
                out[:, at : at + columns] = kept[:, there].astype(f32) + got[:, there].astype(f32)
            at += columns


def finish_feed(groups, counts, columns):
    operands = [part for group in groups for part in (group.kept, group.got)]
    shape = (operands[0].shape[0], sum(counts) * columns)
    return call(
        functools.partial(finish_feed_body, counts=counts, columns=columns),
        "finish_feed",
        (1,),
        [near(part.shape) for part in operands],
        [whole(shape)] * 3,
        [like(shape, f32)] * 3,
        near_in=range(len(operands)),
    )(*operands)


def finish_attention_body(kept, got, proj_kept, proj_got, *outs):
    heads = outs[0].shape[1]
    outs[3][...] = proj_kept[...].astype(f32) + proj_got[...].astype(f32)
    for place, out in enumerate(outs[:3]):
        there = slice(place * heads, place * heads + heads)
        out[...] = kept[:, there].astype(f32) + got[:, there].astype(f32)


def finish_attention(group, proj):
    operands = (group.kept, group.got, proj.kept, proj.got)
    return call(
        finish_attention_body,
        "finish_attention",
        (1,),
        [near(one.shape) for one in operands],
        [whole(proj.kept.shape)] * 4,
        [like(proj.kept.shape, f32)] * 4,
        near_in=range(4),
    )(*operands)


def on_device(
    frames,
    segment_ids,
    w_query,
    w_key,
    w_value,
    w_out,
    w_gate,
    w_up,
    w_down,
    norm1_gain,
    norm1_bias,
    norm2_gain,
    norm2_bias,
    scale_attn,
    scale_mlp,
    output_grad,
):
    Chain.token, Chain.held, Chain.weight = None, [], 0
    paired = lax.axis_size("narrow") == 2
    narrow = lax.axis_index("narrow").astype(jnp.int32)
    wide = Wide()
    rows_own, width = frames.shape
    length = segment_ids.shape[1]
    units = w_gate.shape[1]
    row = lambda vector: vector.reshape(1, -1)
    gain1, bias1, gain2, bias2 = map(row, (norm1_gain, norm1_bias, norm2_gain, norm2_bias))
    scale1, scale2 = row(scale_attn), row(scale_mlp)
    rows_per, span = 128, 128 + 2 * HALF_WINDOW
    core = (narrow if paired else narrow * 0).reshape(1)
    rows_done = length // 2 if paired else length

    def swapped(values):
        return lax.ppermute(values, "narrow", [(0, 1), (1, 0)])

    def both(values):
        return (values, swapped(values)) if paired else (values,)

    def bases(size):
        if paired:
            return [(1 - core) * (rows_done // size), core * (rows_done // size)]
        return [core]

    if paired:
        frame_rows, grad_rows, w_out_all = both(frames), both(output_grad), both(w_out)
    else:
        frame_rows = (lax.all_gather(frames, "narrow", axis=0, tiled=True),)
        grad_rows = (lax.all_gather(output_grad, "narrow", axis=0, tiled=True),)
        w_out_all = (lax.all_gather(w_out, "narrow", axis=0, tiled=True),)
    x, dy = frame_rows[0], grad_rows[0]
    scaled = [cotangent(dy, scale2)]
    q, k, v, cos, sin, clips, normed = project(
        bases(256)[-1], frame_rows, segment_ids, gain1, bias1, w_query, w_key, w_value
    )
    mixed, chances = [], None
    for base in bases(rows_per):
        o_part, chances = attend(
            base, q, k, v, segment_ids, clips, rows_done // rows_per, rows_per, span, chances
        )
        mixed.insert(0, o_part)
    if paired:
        o_all = (mixed[0], swapped(mixed[1]))
    else:
        o_all = (lax.all_gather(mixed[0], "narrow", axis=1, tiled=True),)
    attn, m, mt, *sent = middle(list(zip(o_all, w_out_all)), x, scale1, gain2, bias2, paired)
    m, mt = [m], [mt]
    for block in sent:
        received = swapped(block)
        scaled.append(cotangent(grad_rows[1], scale2, 1))
    for _ in sent:
        turned, copied = turn(received, 1, 1, copies=1)
        m.append(copied)
        mt.append(turned)
    gm, gmt = zip(*scaled)

    def product(lefts, rights, dims, name, own, relative, apart=False):
        if not paired:
            return multiply(core, length, lefts, rights, dims, name, f32)[0]
        other, mine = [core * 0 + rows_done // 256, core * 0] if relative else bases(256)
        place = mine if own else other
        results = multiply(
            place, rows_done, lefts, rights, dims, name, near_out=range(4), apart=apart
        )
        return results if apart else results[0]

    def scattered(part):
        return [lax.psum_scatter(part, "narrow", scatter_dimension=0, tiled=True)]

    columns = min(256, units)
    total = units // columns
    counts, kinds, plan = (COUNTS, KINDS, PLAN) if total == sum(COUNTS) else ([total], ["xyz"] * 3, SHORT)
    here = (narrow * 0 if paired else narrow * (rows_own // min(256, rows_own))).reshape(1)
    groups, hidden, grads, partial, norm2 = {}, [], (), {}, None

    for entry in plan:
        step, _, weight = entry.partition(":")
        Chain.weight += int(weight or 0) * 1150000000
        name, at = step[0], step[1:]
        if name == "F":
            at = int(at)
            where = (w_gate, w_up, w_down, sum(counts[:at]), counts[at], columns)
            sent = 2 if paired and at == len(counts) - 1 else 0
            outs = feed(wide.back(kinds[at]), m, gm, mt, gmt, *where, norm2, sent)
            hidden.append(outs[0])
            groups[str(at)] = Group(wide, kinds[at], *outs[1:3])
            norm2 = outs[3]
            norm2_sent = outs[4:]
            if at == len(counts) - 1 and paired:
                norm2_sent = [swapped(block) for block in norm2_sent]
        elif name == "h":
            groups[at].advance()
        elif name == "e":
            Chain.held = [*Chain.held, groups[at].got]
        elif step == "mb":
            norm2 = [norm2, norm2_sent] if paired else [lax.psum(norm2, "narrow")]
            gh, ga, gat, sums, *sent = middle_back(norm2, x, attn, dy, scale1, gain2, paired)
            if not paired:
                sums = jnp.where(narrow == 0, sums, 0.0)
            ga = [[ga]] + [[swapped(block) for block in sent]] * paired
            gat = [gat]
        elif name == "a":
            at = int(at)
            base = bases(rows_per)[-1 - at]
            last = at == len(ga) - 1
            grads = attend_back(
                base, ga[at], w_out, q, k, v, chances, cos, sin, rows_per, span, grads, last
            )
            gq, gk, gv = grads[:3]
        elif step == "ut":
            ut = [turn(normed, 0, 0, part * rows_done, rows_done) for part in range(1 + paired)]
        elif step == "turn":
            gat += [turn(block, 1, 1) for rows in ga[1:] for block in rows]
        elif step == "w":
            kind = kinds[-1]
            groups["t"] = Group(wide, kind, *attention_weights(core, wide.back(kind), ut, gq, gk, gv))
        elif step == "p":
            kind = kinds[-2]
            groups["p"] = Group(wide, kind, *proj_weights(wide.back(kind), gat, mixed))
        elif step in ("q", "qa", "qb", "o", "oa", "ob"):
            if name == "q":
                args = ([[gq], [gk], [gv]], [w_query, w_key, w_value], NT, "norm1_grad")
            else:
                args = ([hidden], [w_down], NN, "mlp_out")
            if not paired:
                partial[name] = scattered(product(*args, False, name == "o"))
            else:
                part = product(*args, at == "b", name == "o")
                partial.setdefault(name, []).append(part if at == "b" else swapped(part))
        elif step == "in":
            input_grad, more = input_rows(here, partial["q"], frames, gh, gain1)
            sums += more
        elif step == "out":
            output, more = output_rows(
                here, partial["o"], frames, attn, output_grad, scale1, scale2
            )
            sums += more
        elif step == "sum":
            sums = add(sums, swapped(sums)) if paired else lax.psum(sums, "narrow")
        elif name == "s":
            sums = add(sums, wide.along(sums, int(at)))
    for bit in range(4, wide.bits):
        sums = add(sums, wide.along(sums, bit))
        for group in groups.values():
            group.advance()
    attention, proj = groups.pop("t"), groups.pop("p")
    gate_grad, up_grad, down_grad = finish_feed(groups.values(), counts, columns)
    query_grad, key_grad, value_grad, proj_grad = finish_attention(attention, proj)

    return (
        output,
        input_grad,
        query_grad,
        key_grad,
        value_grad,
        proj_grad.T,
        gate_grad,
        up_grad,
        down_grad.T,
        sums[4],
        sums[5],
        sums[0],
        sums[1],
        sums[2],
        sums[3],
    )


def solution(mesh):
    rows = P(("wide", "narrow"), None)
    across = P(None, "narrow")
    return jax.shard_map(
        on_device,
        mesh=mesh,
        in_specs=(rows, P("wide", None))
        + (across,) * 3
        + (P("narrow", None),)
        + (across,) * 2
        + (P("narrow", None),)
        + (P(),) * 6
        + (rows,),
        out_specs=(rows, rows)
        + (P("wide", "narrow"),) * 3
        + (P("narrow", "wide"),)
        + (P("wide", "narrow"),) * 2
        + (P("narrow", "wide"),)
        + (P(),) * 6,
        check_vma=False,
    )
```

```python
import functools
import math

import jax
import jax.numpy as jnp
import numpy as np
from jax import lax
from jax.experimental import pallas as pl
from jax.experimental.pallas import tpu as pltpu
from jax.sharding import PartitionSpec as P

HEAD_DIM = 64
HALF_WINDOW = 64
CLIPS = 6
MAX_CLIP = 384
norm_eps = 1e-05
masked_score = -1e30
COUNTS = [3, 3, 2]
KINDS = ["zy", "zx", "xyz", "xyz", "xyz"]
PLAN = [
    "F0:1", "F1:6", "F2:13", "h0:1", "ut:3", "mb:10", "a0", "turn", "p", "h1", "a1", "h2:1", "oa",
    "w", "ob", "qa:1", "h0:2", "h2", "h1:10", "ht", "h2:2", "out:2", "h1:1", "qb:1", "ht", "in",
    "h0", "hp", "e2:2", "sum", "ht:1", "hp", "s0", "s1", "e1", "s2", "hp", "e0:1", "et", "s3",
    "ep:6",
]
SHORT = ["F0", "ut", "mb", "p", "a0", "w", "h0", "hp", "ht", "q", "o", "h0", "hp", "ht", "in", "out", "sum", "s0", "s1", "s2", "s3", "h0", "hp", "ht"]
bf16 = jnp.bfloat16
f32 = jnp.float32
NN = (((1,), (0,)), ((), ()))
NT = (((1,), (1,)), ((), ()))
TN = (((0,), (0,)), ((), ()))


def dot(a, b, dims=NN):
    return lax.dot_general(a, b, dims, preferred_element_type=f32)


class Chain:
    token = None
    held = []
    weight = 0


def call(
    body,
    name,
    grid,
    in_specs,
    out_specs,
    out_shape,
    scratch=(),
    prefetch=0,
    mib=16,
    aliases=None,
    near_in=(),
    near_out=(),
):
    outputs = len(out_specs)
    before = [] if Chain.token is None else [(Chain.token, pltpu.HBM)]
    before += [(one, pltpu.VMEM) for one in Chain.held]
    Chain.held = []
    extra = len(before)
    weight, Chain.weight = 1 + Chain.weight, 0

    def inner(*refs):
        rest = refs[prefetch + extra :]
        ins = len(in_specs)
        body(*refs[:prefetch], *rest[: ins + outputs], *rest[ins + outputs + 1 :])

    anywhere = pl.BlockSpec(memory_space=pl.ANY)
    shapes = [
        (pltpu.VMEM if at in near_out else pltpu.HBM)(one.shape, one.dtype)
        for at, one in enumerate(out_shape)
    ]
    run = pl.pallas_call(
        inner,
        grid_spec=pltpu.PrefetchScalarGridSpec(
            num_scalar_prefetch=prefetch,
            grid=grid,
            in_specs=[anywhere] * extra + list(in_specs),
            out_specs=list(out_specs) + [anywhere],
            scratch_shapes=list(scratch),
        ),
        out_shape=shapes + [pltpu.HBM((8, 128), f32)],
        input_output_aliases={at + extra: out for at, out in (aliases or {}).items()},
        compiler_params=pltpu.CompilerParams(vmem_limit_bytes=mib * 2**20),
        cost_estimate=pl.CostEstimate(flops=weight, bytes_accessed=1, transcendentals=0),
        name=name,
    )

    def apply(*operands):
        placed = before + [
            (one, pltpu.VMEM if at in near_in else pltpu.HBM)
            for at, one in enumerate(operands[prefetch:])
        ]
        placed = [pltpu.with_memory_space_constraint(*one) for one in placed]
        *results, Chain.token = run(*operands[:prefetch], *placed)
        return results

    return apply


def near(shape):
    return pl.BlockSpec(memory_space=pltpu.VMEM)


def whole(shape):
    return pl.BlockSpec(
        shape, lambda *_: (0,) * len(shape), pipeline_mode=pl.Buffered(1)
    )


def like(shape, kind=bf16):
    return jax.ShapeDtypeStruct(shape, kind)


def normalise(rows):
    centred = rows - jnp.mean(rows, axis=-1, keepdims=True)
    inverse = lax.rsqrt(jnp.mean(centred * centred, axis=-1, keepdims=True) + norm_eps)
    return centred * inverse, inverse


def norm_back(incoming, unit, inverse, gain):
    scaled = incoming * gain
    return inverse * (
        scaled
        - jnp.mean(scaled, axis=-1, keepdims=True)
        - unit * jnp.mean(scaled * unit, axis=-1, keepdims=True)
    )


def rope_table():
    half = HEAD_DIM // 2
    lane = np.arange(128)
    frequency = np.exp((lane % half) * (-math.log(10000.0) / half))
    angle = np.arange(MAX_CLIP)[:, None] * frequency[None, :]
    sign = np.where(lane % HEAD_DIM < half, -1.0, 1.0)
    parts = []
    for table in (np.cos(angle), np.sin(angle) * sign):
        high = table.astype(np.float32).astype(bf16)
        parts += [high, (table - high.astype(np.float64)).astype(np.float32).astype(bf16)]
    return np.concatenate(parts, axis=1)


def swap_halves(values):
    half = HEAD_DIM // 2
    width = values.shape[-1]
    lane = lax.broadcasted_iota(jnp.int32, values.shape, 1)
    return jnp.where(
        lane % HEAD_DIM < half,
        pltpu.roll(values, width - half, 1),
        pltpu.roll(values, half, 1),
    )


def column_of(row, start, count):
    pieces = []
    for place in range(count // 128):
        piece = row[:, pl.ds(pl.multiple_of(start + place * 128, 128), 128)]
        pieces.append(jnp.broadcast_to(piece.astype(f32), (128, 128)).T)
    return jnp.concatenate(pieces, axis=0) if len(pieces) > 1 else pieces[0]


def project_body(base, *refs, parts):
    xs = refs[:parts]
    seg, gain, bias, table, wq, wk, wv, q, k, v, cos, sin, clips, kept = refs[parts:]
    step, blocks = pl.program_id(0), pl.num_programs(0)
    block = lax.rem(base[0] + step, blocks)
    rows_per = xs[0].shape[0]
    raw = xs[0][...]
    for part in range(1, parts):
        raw = jnp.where(step >= part * (blocks // parts), xs[part][...], raw)
    unit, _ = normalise(raw.astype(f32))
    normed = (unit * gain[...] + bias[...]).astype(bf16)
    kept[...] = normed
    ids = seg[...]
    mine = column_of(seg, block * rows_per, rows_per)
    clips[...] = mine
    start = jnp.zeros_like(mine)
    for clip in range(CLIPS - 1):
        count = jnp.sum((ids == clip).astype(f32), axis=-1, keepdims=True)
        start += jnp.where(mine > clip, count, 0.0)
    place = lax.broadcasted_iota(jnp.int32, mine.shape, 0) + block * rows_per
    place = place - start.astype(jnp.int32)
    lane = lax.broadcasted_iota(jnp.int32, mine.shape, 1)
    hot = jnp.concatenate(
        [(place == lane + 128 * part).astype(bf16) for part in range(MAX_CLIP // 128)], axis=1
    )
    rows = dot(hot, table[...])
    cosine = rows[:, :128] + rows[:, 128:256]
    sine = rows[:, 256:384] + rows[:, 384:]
    cos[...] = cosine
    sin[...] = sine
    for weights, out, factor in ((wq, q, HEAD_DIM**-0.5), (wk, k, 1.0)):
        flat = dot(normed, weights[...])
        for at in range(0, flat.shape[1], 128):
            part = flat[:, at : at + 128]
            part = part * cosine + swap_halves(part) * sine
            out[:, at : at + 128] = (part * factor).astype(bf16)
    v[...] = dot(normed, wv[...]).astype(bf16)


def project(base, xs, seg, gain, bias, wq, wk, wv, rows_per=256):
    parts = len(xs)
    each, width = xs[0].shape
    length = parts * each
    heads = wq.shape[1]
    blocks = length // rows_per

    def out(columns):
        return pl.BlockSpec((rows_per, columns), lambda i, base: (lax.rem(base[0] + i, blocks), 0))

    def piece(part):
        count = each // rows_per
        return pl.BlockSpec(
            (rows_per, width), lambda i, base: (jnp.clip(i - part * count, 0, count - 1), 0)
        )

    table = rope_table()
    return call(
        functools.partial(project_body, parts=parts),
        "project",
        (blocks,),
        [piece(part) for part in range(parts)]
        + [
            whole(seg.shape),
            whole((1, width)),
            whole((1, width)),
            whole(table.shape),
            whole(wq.shape),
            whole(wk.shape),
            whole(wv.shape),
        ],
        [out(heads)] * 3
        + [out(128)] * 3
        + [pl.BlockSpec((rows_per, width), lambda i, base: (i, 0))],
        [like((length, heads))] * 3 + [like((length, 128), f32)] * 3 + [like((length, width))],
        prefetch=1,
        near_out=[0, 1, 2, 5],
    )(base, *xs, seg, gain, bias, jnp.asarray(table), wq, wk, wv)


def band(block, rows_per, span, length):
    first = block * rows_per
    start = jnp.clip(first - HALF_WINDOW, 0, length - span)
    return first, pl.multiple_of(start, HALF_WINDOW)


def two_heads(values):
    lane = lax.broadcasted_iota(jnp.int32, values.shape, 1)
    zero = jnp.zeros_like(values)
    return jnp.concatenate(
        [jnp.where(lane < HEAD_DIM, values, zero), jnp.where(lane < HEAD_DIM, zero, values)], axis=0
    )


def one_each(stacked):
    count = stacked.shape[0] // 2
    lane = lax.broadcasted_iota(jnp.int32, (count, 128), 1)
    return jnp.where(lane < HEAD_DIM, stacked[:count], stacked[count:])


def attend_body(base, q, k, v, seg, clips, *refs, span):
    o, weights = refs[-2:]
    rows_per = q.shape[0]
    length = k.shape[0]
    block = base[0] + pl.program_id(0)
    first, start = band(block, rows_per, span, length)
    mine = seg[:, pl.ds(first, rows_per)]
    theirs = clips[pl.ds(start, span), :]
    gap = (
        lax.broadcasted_iota(jnp.int32, (span, rows_per), 0)
        - lax.broadcasted_iota(jnp.int32, (span, rows_per), 1)
        + (start - first)
    )
    allowed = (gap >= -HALF_WINDOW) & (gap < HALF_WINDOW) & (theirs == mine.astype(f32))
    penalty = jnp.where(allowed, 0.0, masked_score)
    penalty = jnp.concatenate([penalty, penalty], axis=1)
    for pair in range(q.shape[1] // 128):
        lanes = slice(pair * 128, pair * 128 + 128)
        keys = k[pl.ds(start, span), lanes]
        values = v[pl.ds(start, span), lanes]
        scores = dot(keys, two_heads(q[:, lanes]), NT) + penalty
        lifted = jnp.exp(scores - jnp.max(scores, axis=0, keepdims=True))
        chances = (lifted * (1.0 / jnp.sum(lifted, axis=0, keepdims=True))).astype(bf16)
        weights[0, pair] = chances
        o[:, lanes] = one_each(dot(chances, values, TN)).astype(bf16)


def attend(base, q, k, v, seg, clips, blocks, rows_per, span, weights=None):
    length, heads = q.shape
    pairs = heads // 128
    kept = [] if weights is None else [weights]
    return call(
        functools.partial(attend_body, span=span),
        "attend",
        (blocks,),
        [
            pl.BlockSpec((rows_per, heads), lambda i, base: (base[0] + i, 0)),
            near(k.shape),
            near(v.shape),
            whole(seg.shape),
            near(clips.shape),
        ]
        + [pl.BlockSpec(memory_space=pl.ANY)] * len(kept),
        [
            pl.BlockSpec((rows_per, heads), lambda i, base: (i, 0)),
            pl.BlockSpec((1, pairs, span, 2 * rows_per), lambda i, base: (base[0] + i, 0, 0, 0)),
        ],
        [like((blocks * rows_per, heads)), like((length // rows_per, pairs, span, 2 * rows_per))],
        prefetch=1,
        aliases={6: 1} if kept else None,
        near_in=[0, 1, 2, 4],
    )(base, q, k, v, seg, clips, *kept)


def attend_back_body(base, *refs, parts, span, start, last):
    ga, wo, q, k, v, weights, cos, sin, *refs = refs[:parts], *refs[parts:]
    gq, gk, gv, acc_k, acc_v = refs[-5:]
    rows_per = q.shape[0]
    length = k.shape[0]
    block = base[0] + pl.program_id(0)
    _, first = band(block, rows_per, span, length)

    if start:

        @pl.when(pl.program_id(0) == 0)
        def _():
            acc_k[...] = jnp.zeros_like(acc_k)
            acc_v[...] = jnp.zeros_like(acc_v)

    rows = ga[0][...]
    for part in range(1, parts):
        rows = jnp.where(pl.program_id(0) >= part * (pl.num_programs(0) // parts), ga[part][...], rows)
    go = dot(rows, wo[...], NT).astype(bf16)
    mine = pl.ds(pl.multiple_of(block * rows_per, rows_per), rows_per)
    cosine, sine = cos[mine, :], sin[mine, :]
    keys_at = pl.ds(first, span)
    for pair in range(q.shape[1] // 128):
        lanes = slice(pair * 128, pair * 128 + 128)
        keys = k[keys_at, lanes]
        values = v[keys_at, lanes]
        chances = weights[0, pair]
        full = chances.astype(f32)
        go_two = two_heads(go[:, lanes])
        change = dot(values, go_two, NT)
        weighted = jnp.sum(full * change, axis=0, keepdims=True)
        gs = (full * (change - weighted)).astype(bf16)
        gq_rows = one_each(dot(gs, keys, TN)) * HEAD_DIM**-0.5
        gq[:, lanes] = (gq_rows * cosine - swap_halves(gq_rows) * sine).astype(bf16)
        acc_k[keys_at, lanes] += dot(gs, two_heads(q[:, lanes]))
        acc_v[keys_at, lanes] += dot(chances, go_two)

    if last:

        @pl.when(pl.program_id(0) == pl.num_programs(0) - 1)
        def _():
            @pl.loop(0, length // rows_per)
            def _(at):
                here = pl.ds(pl.multiple_of(at * rows_per, rows_per), rows_per)
                gv[here, :] = acc_v[here, :].astype(bf16)
                for pair in range(q.shape[1] // 128):
                    lanes = slice(pair * 128, pair * 128 + 128)
                    rows = acc_k[here, lanes]
                    rows = rows * cos[here, :] - swap_halves(rows) * sin[here, :]
                    gk[here, lanes] = rows.astype(bf16)


def attend_back(base, ga, wo, q, k, v, weights, cos, sin, rows_per, span, kept, last):
    length, heads = q.shape
    pairs = heads // 128
    parts = len(ga)
    each, width = ga[0].shape
    rows = parts * each
    row = pl.BlockSpec((rows_per, heads), lambda i, base: (base[0] + i, 0))
    full = near((length, heads))

    def block(part):
        count = each // rows_per
        return pl.BlockSpec(
            (rows_per, width), lambda i, base: (jnp.clip(i - part * count, 0, count - 1), 0)
        )

    return call(
        functools.partial(
            attend_back_body, parts=parts, span=span, start=not kept, last=last
        ),
        "attend_back",
        (rows // rows_per,),
        [block(part) for part in range(parts)]
        + [
            whole(wo.shape),
            row,
            full,
            full,
            pl.BlockSpec((1, pairs, span, 2 * rows_per), lambda i, base: (base[0] + i, 0, 0, 0)),
            whole(cos.shape),
            whole(sin.shape),
        ]
        + [full if at > 0 else pl.BlockSpec(memory_space=pl.ANY) for at in range(len(kept))],
        [row, full, full, full, full],
        [like((length, heads))] * 3 + [like((length, heads), f32)] * 2,
        prefetch=1,
        aliases={8 + parts + at: at for at in range(len(kept))},
        near_in=list(range(parts))
        + [parts + at for at in (1, 2, 3)]
        + [parts + 7 + at for at in range(len(kept))],
        near_out=range(5),
    )(base, *ga, wo, q, k, v, weights, cos, sin, *kept)


def put_transposed(target, values):
    for at in range(0, values.shape[1], 128):
        target[at : at + 128, :] = values[:, at : at + 128].T


def cotangent_body(dy, scale, gm, gmt):
    scaled = (dy[...].astype(f32) * scale[...]).astype(bf16)
    gm[...] = scaled
    put_transposed(gmt, scaled)


def cotangent(dy, scale, near_in=0, rows_per=256):
    rows, width = dy.shape
    row = pl.BlockSpec((rows_per, width), lambda i: (i, 0))
    return call(
        cotangent_body,
        "cotangent",
        (rows // rows_per,),
        [row, whole((1, width))],
        [row, pl.BlockSpec((width, rows_per), lambda i: (0, i))],
        [like((rows, width)), like((width, rows))],
        near_in=range(near_in),
        near_out=range(2 * near_in),
    )(dy, scale)


def place_body(received, own, own_turned, turned, *copies):
    put_transposed(turned, received[...])
    for copy, values in zip(copies, (received, own, own_turned)):
        copy[...] = values[...]


def place(received, own, own_turned, rows_per=256):
    length, width = received.shape
    row = pl.BlockSpec((rows_per, width), lambda i: (i, 0))
    column = pl.BlockSpec((width, rows_per), lambda i: (0, i))
    return call(
        place_body,
        "place",
        (length // rows_per,),
        [row, row, column],
        [column, row, row, column],
        [like((width, length)), like((length, width)), like((length, width)), like((width, length))],
        near_in=range(1),
        near_out=range(4),
    )(received, own, own_turned)


def turn_body(values, out):
    put_transposed(out, values[...])


def turn(values, near_in=0, near_out=0, start=0, length=None, rows_per=256):
    width = values.shape[1]
    length = length or values.shape[0]
    rows_per = min(rows_per, length)
    first = start // rows_per
    return call(
        turn_body,
        "turn",
        (length // rows_per,),
        [pl.BlockSpec((rows_per, width), lambda i: (i + first, 0))],
        [pl.BlockSpec((width, rows_per), lambda i: (0, i))],
        [like((width, length))],
        near_in=range(near_in),
        near_out=range(near_out),
    )(values)[0]


def middle_body(*refs, parts):
    mixed = refs[: 2 * parts]
    x, scale, gain, bias = refs[2 * parts : 2 * parts + 4]
    attn, m, mt, *sent = refs[2 * parts + 4 :]
    total = dot(mixed[0][...], mixed[1][...])
    for part in range(1, parts):
        total += dot(mixed[2 * part][...], mixed[2 * part + 1][...])
    low = total.astype(bf16)
    attn[...] = low
    rows = x[...].astype(f32) + scale[...] * low.astype(f32)
    unit, _ = normalise(rows)
    normed = (unit * gain[...] + bias[...]).astype(bf16)
    m[...] = normed
    put_transposed(mt, normed)
    for copy in sent:
        copy[...] = normed


def middle(mixed, x, scale, gain, bias, sent, rows_per=256):
    rows, width = x.shape
    specs, operands = [], []
    for left, right in mixed:
        specs += [
            pl.BlockSpec((rows_per, left.shape[1]), lambda i: (i, 0)),
            whole(right.shape),
        ]
        operands += [left, right]
    row = pl.BlockSpec((rows_per, width), lambda i: (i, 0))
    return call(
        functools.partial(middle_body, parts=len(mixed)),
        "middle",
        (rows // rows_per,),
        specs + [row, whole((1, width)), whole((1, width)), whole((1, width))],
        [row, row, pl.BlockSpec((width, rows_per), lambda i: (0, i))] + [row] * sent,
        [like((rows, width)), like((rows, width)), like((width, rows))]
        + [like((rows, width))] * sent,
        near_in=[2, 3] * (len(mixed) > 1),
    )(*operands, x, scale, gain, bias)


def gathered(source, back, quarter, piece):
    groups = source.shape[0] // (4 * piece)
    return jnp.concatenate(
        [
            source[pl.ds(pl.multiple_of(back[quarter * groups + at] * piece, piece), piece), :]
            for at in range(groups)
        ],
        axis=0,
    )


def put_quarter(sent, kept, quarter, start, values):
    height = values.shape[0]
    place = slice((quarter % 2) * height, (quarter % 2) * height + height)
    (sent if quarter < 2 else kept)[place, start : start + values.shape[1]] = values


def feed_grads_body(back, *refs, parts):
    mt, gmt = refs[:parts], refs[parts : 2 * parts]
    hid, gg, gu, sent, kept = refs[2 * parts :]
    piece = gmt[0].shape[0] // back.shape[0]
    columns = hid.shape[1]
    each = gmt[0].shape[1]

    def product(lefts, right):
        total = dot(lefts[0], right[:each, :])
        for part in range(1, parts):
            total += dot(lefts[part], right[part * each : part * each + each, :])
        return total.astype(bf16)

    for quarter in range(4):
        grad_rows = [gathered(source, back, quarter, piece) for source in gmt]
        put_quarter(sent, kept, quarter, 0, product(grad_rows, hid))
        rows = [gathered(source, back, quarter, piece) for source in mt]
        put_quarter(sent, kept, quarter, columns, product(rows, gg))
        put_quarter(sent, kept, quarter, 2 * columns, product(rows, gu))


def feed_acts_body(m, gm, wg, wu, wd, hid, gg, gu, total, fresh, rows_per):
    each = m[0].shape[0]
    for part in range(len(m)):

        @pl.loop(0, each // rows_per)
        def _(at, part=part):
            here = pl.ds(pl.multiple_of(at * rows_per, rows_per), rows_per)
            there = pl.ds(pl.multiple_of(part * each + at * rows_per, rows_per), rows_per)
            rows = m[part][here, :]
            gate = dot(rows, wg[...])
            up = dot(rows, wu[...])
            back = dot(gm[part][here, :], wd[...], NT)
            sigma = 1.0 / (1.0 + jnp.exp(-gate))
            active = gate * sigma
            hid[there, :] = (active * up).astype(bf16)
            gate_back = (back * up * sigma * (1.0 + gate * (1.0 - sigma))).astype(bf16)
            up_back = (back * active).astype(bf16)
            gg[there, :] = gate_back
            gu[there, :] = up_back
            both = jnp.concatenate([gate_back, up_back], axis=1)
            for start in range(0, total.shape[1], 256):
                cols = slice(start, start + 256)
                weights = jnp.concatenate([wg[cols, :], wu[cols, :]], axis=1)
                more = dot(both, weights, NT)
                total[there, cols] = jnp.where(fresh, more, total[there, cols] + more)


def feed_body(back, *refs, parts, rows_per, first, sent_blocks):
    m, gm, mt, gmt = (refs[at * parts : (at + 1) * parts] for at in range(4))
    wg, wu, wd, *refs = refs[4 * parts :]
    gg, gu = refs[-2:]
    hid, sent, kept, total, *blocks = refs[-6 - sent_blocks : -2]
    step = pl.program_id(0)
    if first:
        start = step == 0
    else:
        start = step < 0

    feed_acts_body(m, gm, wg, wu, wd, hid, gg, gu, total, start, rows_per)
    feed_grads_body(back, *mt, *gmt, hid, gg, gu, sent, kept, parts=parts)
    if blocks:

        @pl.when(step == pl.num_programs(0) - 1)
        def _():
            height = blocks[0].shape[0]
            base = total.shape[0] // 2
            for at, out in enumerate(blocks):
                out[...] = total[base + at * height : base + at * height + height, :].astype(bf16)


def feed(back, m, gm, mt, gmt, wg, wu, wd, first, count, columns, total, sent_blocks, rows_per=512):
    each, width = gm[0].shape
    parts = len(gm)
    length = each * parts
    col = pl.BlockSpec((width, columns), lambda j, back: (0, j + first))
    out = pl.BlockSpec((length, columns), lambda j, back: (0, j))
    grad = pl.BlockSpec((width // 2, 3 * columns), lambda j, back: (0, j))
    so_far = [] if total is None else [total]
    block = (length // 2 // max(sent_blocks, 1), width)
    return call(
        functools.partial(
            feed_body, parts=parts, rows_per=rows_per, first=total is None, sent_blocks=sent_blocks
        ),
        "feed",
        (count,),
        [near((each, width))] * (4 * parts)
        + [col, col, pl.BlockSpec((columns, width), lambda j, back: (j + first, 0))]
        + [near((length, width))] * len(so_far),
        [out] + [grad] * 2 + [near((length, width))] + [whole(block)] * sent_blocks,
        [like((length, columns * count))]
        + [like((width // 2, 3 * columns * count))] * 2
        + [like((length, width), f32)]
        + [like(block)] * sent_blocks,
        scratch=[pltpu.VMEM((length, columns), bf16)] * 2,
        prefetch=1,
        near_in=list(range(4 * parts)) + [4 * parts + 3] * len(so_far),
        near_out=range(1, 4 + sent_blocks),
        aliases={4 * parts + 4: 3} if so_far else None,
        mib=24,
    )(back, *m, *gm, *mt, *gmt, wg, wu, wd, *so_far)


def multiply_body(base, *refs, counts, dims):
    lefts, rights = refs[: sum(counts)], refs[sum(counts) : sum(counts) + len(counts)]
    outs = refs[sum(counts) + len(counts) :]
    total = None
    piece = 0
    for count, right in zip(counts, rights):
        at = 0
        for left in lefts[piece : piece + count]:
            depth = left.shape[1]
            if dims is NN:
                part = dot(left[...], right[at : at + depth, :])
            else:
                part = dot(left[...], right[:, at : at + depth], NT)
            total = part if total is None else total + part
            at += depth
        piece += count
    total = total.astype(outs[0].dtype)
    if len(outs) == 1:
        outs[0][...] = total
        return
    for block, out in enumerate(outs):

        @pl.when(pl.program_id(0) == block)
        def _(out=out):
            out[...] = total


def multiply(base, rows, lefts, rights, dims, name, kind=bf16, rows_per=256, near_in=(), near_out=(), apart=False):
    width = rights[0].shape[1 if dims is NN else 0]
    pieces = [piece for left in lefts for piece in left]
    return call(
        functools.partial(multiply_body, counts=[len(left) for left in lefts], dims=dims),
        name,
        (rows // rows_per,),
        [
            pl.BlockSpec((rows_per, piece.shape[1]), lambda i, base: (base[0] + i, 0))
            for piece in pieces
        ]
        + [whole(right.shape) for right in rights],
        [whole((rows_per, width))] * (rows // rows_per)
        if apart
        else [pl.BlockSpec((rows_per, width), lambda i, base: (i, 0))],
        [like((rows_per, width), kind)] * (rows // rows_per)
        if apart
        else [like((rows, width), kind)],
        prefetch=1,
        mib=24,
        near_in=near_in,
        near_out=near_out,
    )(base, *pieces, *rights)


def middle_back_body(*refs, parts):
    pieces = sum(parts)
    x, attn, dy, scale, gain, gh, ga, gat, sums, *sent = refs[pieces:]
    step = pl.program_id(0)
    incoming = None
    at = 0
    for count in parts:
        rows = refs[at][...].astype(f32)
        for block in range(1, count):
            rows = jnp.where(step == block, refs[at + block][...].astype(f32), rows)
        incoming = rows if incoming is None else incoming + rows
        at += count
    attn_rows = attn[...].astype(f32)
    unit, inverse = normalise(x[...].astype(f32) + scale[...] * attn_rows)
    grad = dy[...].astype(f32) + norm_back(incoming, unit, inverse, gain[...])
    gh[...] = grad
    low = (scale[...] * grad).astype(bf16)
    ga[...] = low
    for block, out in enumerate(sent):

        @pl.when(step == block)
        def _(out=out):
            out[...] = low

    put_transposed(gat, low)

    @pl.when(step == 0)
    def _():
        sums[...] = jnp.zeros_like(sums)

    sums[0:1, :] += jnp.sum(incoming * unit, axis=0, keepdims=True)
    sums[1:2, :] += jnp.sum(incoming, axis=0, keepdims=True)
    sums[2:3, :] += jnp.sum(attn_rows * grad, axis=0, keepdims=True)


def middle_back(partial, x, attn, dy, scale, gain, sent, rows_per=256):
    rows, width = x.shape
    blocks = rows // rows_per
    row = pl.BlockSpec((rows_per, width), lambda i: (i, 0))
    partial = [part if isinstance(part, list) else [part] for part in partial]
    specs = [
        row if len(part) == 1 else whole((rows_per, width)) for part in partial for _ in part
    ]
    flat = [block for part in partial for block in part]
    return call(
        functools.partial(middle_back_body, parts=[len(part) for part in partial]),
        "middle_back",
        (blocks,),
        specs + [row, row, row, whole((1, width)), whole((1, width))],
        [
            row,
            row,
            pl.BlockSpec((width, rows_per), lambda i: (0, i)),
            whole((8, width)),
        ]
        + [whole((rows_per, width))] * (blocks * sent),
        [
            like((rows, width), f32),
            like((rows, width)),
            like((width, rows)),
            like((8, width), f32),
        ]
        + [like((rows_per, width))] * (blocks * sent),
        near_in=range(len(flat)),
        near_out=[1, 2] + list(range(4, 4 + blocks * sent)),
    )(*flat, x, attn, dy, scale, gain)


def weights_body(core, back, *refs, parts):
    ut, (gq, gk, gv, sent, kept) = refs[:parts], refs[parts:]
    piece = ut[0].shape[0] // back.shape[0]
    each = ut[0].shape[1]
    heads = gq.shape[1]

    def product(lefts, right):
        total = None
        for part in range(parts):
            first = (core[0] if part == 0 else 1 - core[0]) * each if parts == 2 else 0
            there = pl.ds(pl.multiple_of(first, each), each) if parts == 2 else slice(None)
            one = dot(lefts[part], right[there, :])
            total = one if total is None else total + one
        return total.astype(bf16)

    for quarter in range(4):
        rows = [gathered(source, back, quarter, piece) for source in ut]
        for place, right in enumerate((gq, gk, gv)):
            put_quarter(sent, kept, quarter, place * heads, product(rows, right))


def attention_weights(core, back, ut, gq, gk, gv):
    width = ut[0].shape[0]
    shape = (width // 2, 3 * gq.shape[1])
    operands = (*ut, gq, gk, gv)
    parts = len(ut)
    close = [parts + at for at in range(3)]
    return call(
        functools.partial(weights_body, parts=parts),
        "attention_weights",
        (1,),
        [(near if at in close else whole)(one.shape) for at, one in enumerate(operands)],
        [near(shape)] * 2,
        [like(shape)] * 2,
        prefetch=2,
        near_in=close,
        near_out=range(2),
    )(core, back, *operands)


def proj_body(back, *refs, parts, blocks):
    gat, o, (sent, kept) = refs[:blocks], refs[blocks : blocks + parts], refs[blocks + parts :]
    piece = gat[0].shape[0] // back.shape[0]
    each = o[0].shape[0]
    for quarter in range(4):
        proj = None
        at = 0
        for block in gat:
            size = block.shape[1]
            right = o[at // each][at % each : at % each + size, :]
            one = dot(gathered(block, back, quarter, piece), right)
            proj = one if proj is None else proj + one
            at += size
        put_quarter(sent, kept, quarter, 0, proj.astype(bf16))


def proj_weights(back, gat, o):
    shape = (gat[0].shape[0] // 2, o[0].shape[1])
    parts, blocks = len(o), len(gat)
    return call(
        functools.partial(proj_body, parts=parts, blocks=blocks),
        "proj_weights",
        (1,),
        [near(one.shape) for one in gat] + [whole(one.shape) for one in o],
        [near(shape)] * 2,
        [like(shape)] * 2,
        prefetch=1,
        near_in=range(blocks),
        near_out=range(2),
    )(back, *gat, *o)


def output_body(core, *refs, parts):
    partial = refs[:parts]
    x, attn, dy, scale_attn, scale_mlp, out, sums = refs[parts:]
    total = partial[0][...].astype(f32)
    for part in range(1, parts):
        total += partial[part][...].astype(f32)
    middle_rows = x[...].astype(f32) + scale_attn[...] * attn[...].astype(f32)
    out[...] = (middle_rows + scale_mlp[...] * total).astype(bf16)

    @pl.when(pl.program_id(0) == 0)
    def _():
        sums[...] = jnp.zeros_like(sums)

    sums[3:4, :] += jnp.sum(total * dy[...].astype(f32), axis=0, keepdims=True)


def output_rows(core, partial, x, attn, dy, scale_attn, scale_mlp, rows_per=256):
    rows, width = x.shape
    rows_per = min(rows_per, rows)
    row = pl.BlockSpec((rows_per, width), lambda i, core: (i, 0))
    own = pl.BlockSpec((rows_per, width), lambda i, core: (i + core[0], 0))
    return call(
        functools.partial(output_body, parts=len(partial)),
        "output_rows",
        (rows // rows_per,),
        [row] * len(partial) + [row, own, row] + [whole((1, width))] * 2,
        [row, whole((8, width))],
        [like((rows, width)), like((8, width), f32)],
        prefetch=1,
        near_in=range(len(partial)),
    )(core, *partial, x, attn, dy, scale_attn, scale_mlp)


def input_body(core, *refs, parts):
    partial = refs[:parts]
    x, gh, gain, out, sums = refs[parts:]
    incoming = partial[0][...].astype(f32)
    for part in range(1, parts):
        incoming += partial[part][...].astype(f32)
    unit, inverse = normalise(x[...].astype(f32))
    out[...] = (gh[...] + norm_back(incoming, unit, inverse, gain[...])).astype(bf16)

    @pl.when(pl.program_id(0) == 0)
    def _():
        sums[...] = jnp.zeros_like(sums)

    sums[4:5, :] += jnp.sum(incoming * unit, axis=0, keepdims=True)
    sums[5:6, :] += jnp.sum(incoming, axis=0, keepdims=True)


def input_rows(core, partial, x, gh, gain, rows_per=256):
    rows, width = x.shape
    rows_per = min(rows_per, rows)
    row = pl.BlockSpec((rows_per, width), lambda i, core: (i, 0))
    own = pl.BlockSpec((rows_per, width), lambda i, core: (i + core[0], 0))
    return call(
        functools.partial(input_body, parts=len(partial)),
        "input_rows",
        (rows // rows_per,),
        [row] * len(partial) + [row, own] + [whole((1, width))],
        [row, whole((8, width))],
        [like((rows, width)), like((8, width), f32)],
        prefetch=1,
        near_in=range(len(partial)),
    )(core, *partial, x, gh, gain)


class Wide:
    def __init__(self):
        self.size = lax.axis_size("wide")
        self.bits = self.size.bit_length() - 1
        assert self.size == 1 << self.bits and self.bits > 2
        self.place = lax.axis_index("wide").astype(jnp.int32)
        self.cores = lax.axis_size("narrow")
        self.core = lax.axis_index("narrow")

    def orders(self, kind):
        rest = list(range(2, self.bits))
        near_far, far_near = [0, 1] + rest, [1, 0] + rest
        return {
            "xyz": (near_far, far_near),
            "zy": (near_far, rest + [1, 0]),
            "zx": (rest + [0, 1], far_near),
            "mid": ([0] + rest + [1], [1] + rest + [0]),
        }[kind]

    def back(self, kind):
        found = []
        for order in self.orders(kind):
            groups = []
            for place in range(self.size):
                apart = 0
                for step, bit in enumerate(order):
                    apart |= (1 - ((place >> (self.bits - 1 - step)) & 1)) << bit
                groups.append(apart)
            found.append(jnp.array(groups, jnp.int32))
        return self.place ^ jnp.where(self.core % 2 == 0, *found)

    def hop(self, values, kind, step):
        orders = self.orders(kind)
        pairs = []
        for group in range(self.size):
            for core in range(self.cores):
                target = group ^ (1 << orders[core % 2][step])
                pairs.append((group * self.cores + core, target * self.cores + core))
        return lax.ppermute(values, ("wide", "narrow"), pairs)

    def along(self, values, bit):
        return lax.ppermute(values, "wide", [(i, i ^ (1 << bit)) for i in range(self.size)])


class Group:
    def __init__(self, wide, kind, sent, kept):
        self.wide, self.kind, self.step = wide, kind, 0
        self.kept, self.got = kept, wide.hop(sent, kind, 0)

    def advance(self):
        sent, self.kept = add_again(self.kept, self.got)
        self.step += 1
        self.got = self.wide.hop(sent, self.kind, self.step)


def add_body(left, right, out):
    out[...] = left[...] + right[...]


def add(left, right):
    return call(
        add_body,
        "add",
        (),
        [near(left.shape)] * 2,
        [near(left.shape)],
        [like(left.shape, left.dtype)],
        near_in=range(2),
        near_out=range(1),
    )(left, right)[0]


def add_again_body(keep, got, sent, rest):
    half = sent.shape[0]
    sent[...] = keep[:half, :] + got[:half, :]
    rest[...] = keep[half:, :] + got[half:, :]


def add_again(keep, got):
    shape = (keep.shape[0] // 2, keep.shape[1])
    return call(
        add_again_body,
        "add_again",
        (),
        [near(keep.shape)] * 2,
        [near(shape)] * 2,
        [like(shape)] * 2,
        near_in=range(2),
        near_out=range(2),
    )(keep, got)


def finish_feed_body(*refs, counts, columns):
    gate, up, down = refs[-3:]
    at = 0
    for group, count in enumerate(counts):
        kept, got = refs[2 * group : 2 * group + 2]
        for block in range(count):
            for part, out in enumerate((down, gate, up)):
                there = slice((3 * block + part) * columns, (3 * block + part + 1) * columns)
                out[:, at : at + columns] = kept[:, there].astype(f32) + got[:, there].astype(f32)
            at += columns


def finish_feed(groups, counts, columns):
    operands = [part for group in groups for part in (group.kept, group.got)]
    shape = (operands[0].shape[0], sum(counts) * columns)
    return call(
        functools.partial(finish_feed_body, counts=counts, columns=columns),
        "finish_feed",
        (1,),
        [near(part.shape) for part in operands],
        [whole(shape)] * 3,
        [like(shape, f32)] * 3,
        near_in=range(len(operands)),
    )(*operands)


def finish_attention_body(kept, got, proj_kept, proj_got, *outs):
    heads = outs[0].shape[1]
    outs[3][...] = proj_kept[...].astype(f32) + proj_got[...].astype(f32)
    for place, out in enumerate(outs[:3]):
        there = slice(place * heads, place * heads + heads)
        out[...] = kept[:, there].astype(f32) + got[:, there].astype(f32)


def finish_attention(group, proj):
    operands = (group.kept, group.got, proj.kept, proj.got)
    return call(
        finish_attention_body,
        "finish_attention",
        (1,),
        [near(one.shape) for one in operands],
        [whole(proj.kept.shape)] * 4,
        [like(proj.kept.shape, f32)] * 4,
        near_in=range(4),
    )(*operands)


def on_device(
    frames,
    segment_ids,
    w_query,
    w_key,
    w_value,
    w_out,
    w_gate,
    w_up,
    w_down,
    norm1_gain,
    norm1_bias,
    norm2_gain,
    norm2_bias,
    scale_attn,
    scale_mlp,
    output_grad,
):
    Chain.token, Chain.held, Chain.weight = None, [], 0
    paired = lax.axis_size("narrow") == 2
    narrow = lax.axis_index("narrow").astype(jnp.int32)
    wide = Wide()
    rows_own, width = frames.shape
    length = segment_ids.shape[1]
    units = w_gate.shape[1]
    row = lambda vector: vector.reshape(1, -1)
    gain1, bias1, gain2, bias2 = map(row, (norm1_gain, norm1_bias, norm2_gain, norm2_bias))
    scale1, scale2 = row(scale_attn), row(scale_mlp)
    rows_per, span = 128, 128 + 2 * HALF_WINDOW
    core = (narrow if paired else narrow * 0).reshape(1)
    rows_done = length // 2 if paired else length

    def swapped(values):
        return lax.ppermute(values, "narrow", [(0, 1), (1, 0)])

    def both(values):
        return (values, swapped(values)) if paired else (values,)

    def bases(size):
        if paired:
            return [(1 - core) * (rows_done // size), core * (rows_done // size)]
        return [core]

    if paired:
        frame_rows, grad_rows, w_out_all = both(frames), both(output_grad), both(w_out)
    else:
        frame_rows = (lax.all_gather(frames, "narrow", axis=0, tiled=True),)
        grad_rows = (lax.all_gather(output_grad, "narrow", axis=0, tiled=True),)
        w_out_all = (lax.all_gather(w_out, "narrow", axis=0, tiled=True),)
    x, dy = frame_rows[0], grad_rows[0]
    scaled = [cotangent(dy, scale2)]
    q, k, v, cos, sin, clips, normed = project(
        bases(256)[-1], frame_rows, segment_ids, gain1, bias1, w_query, w_key, w_value
    )
    mixed, chances = [], None
    for base in bases(rows_per):
        o_part, chances = attend(
            base, q, k, v, segment_ids, clips, rows_done // rows_per, rows_per, span, chances
        )
        mixed.insert(0, o_part)
    if paired:
        o_all = (mixed[0], swapped(mixed[1]))
    else:
        o_all = (lax.all_gather(mixed[0], "narrow", axis=1, tiled=True),)
    attn, m, mt, *sent = middle(list(zip(o_all, w_out_all)), x, scale1, gain2, bias2, paired)
    m, mt = (m,), (mt,)
    for block in sent:
        received = swapped(block)
        scaled.append(cotangent(grad_rows[1], scale2, 1))
        turned, *copies = place(received, m[0], mt[0])
        m, mt = (copies[1], copies[0]), (copies[2], turned)
    gm, gmt = zip(*scaled)

    def product(lefts, rights, dims, name, own, relative, apart=False):
        if not paired:
            return multiply(core, length, lefts, rights, dims, name, f32)[0]
        other, mine = [core * 0 + rows_done // 256, core * 0] if relative else bases(256)
        place = mine if own else other
        results = multiply(
            place, rows_done, lefts, rights, dims, name, near_out=range(4), apart=apart
        )
        return results if apart else results[0]

    def scattered(part):
        return [lax.psum_scatter(part, "narrow", scatter_dimension=0, tiled=True)]

    columns = min(256, units)
    total = units // columns
    counts, kinds, plan = (COUNTS, KINDS, PLAN) if total == sum(COUNTS) else ([total], ["xyz"] * 3, SHORT)
    here = (narrow * 0 if paired else narrow * (rows_own // min(256, rows_own))).reshape(1)
    groups, hidden, grads, partial, norm2 = {}, [], (), {}, None

    for entry in plan:
        step, _, weight = entry.partition(":")
        Chain.weight += int(weight or 0) * 1150000000
        name, at = step[0], step[1:]
        if name == "F":
            at = int(at)
            where = (w_gate, w_up, w_down, sum(counts[:at]), counts[at], columns)
            sent = 2 if paired and at == len(counts) - 1 else 0
            outs = feed(wide.back(kinds[at]), m, gm, mt, gmt, *where, norm2, sent)
            hidden.append(outs[0])
            groups[str(at)] = Group(wide, kinds[at], *outs[1:3])
            norm2 = outs[3]
            norm2_sent = outs[4:]
            if at == len(counts) - 1 and paired:
                norm2_sent = [swapped(block) for block in norm2_sent]
        elif name == "h":
            groups[at].advance()
        elif name == "e":
            Chain.held = [*Chain.held, groups[at].got]
        elif step == "mb":
            norm2 = [norm2, norm2_sent] if paired else [lax.psum(norm2, "narrow")]
            gh, ga, gat, sums, *sent = middle_back(norm2, x, attn, dy, scale1, gain2, paired)
            if not paired:
                sums = jnp.where(narrow == 0, sums, 0.0)
            ga = [[ga]] + [[swapped(block) for block in sent]] * paired
            gat = [gat]
        elif name == "a":
            at = int(at)
            base = bases(rows_per)[-1 - at]
            last = at == len(ga) - 1
            grads = attend_back(
                base, ga[at], w_out, q, k, v, chances, cos, sin, rows_per, span, grads, last
            )
            gq, gk, gv = grads[:3]
        elif step == "ut":
            ut = [turn(normed, 0, 0, part * rows_done, rows_done) for part in range(1 + paired)]
        elif step == "turn":
            gat += [turn(block, 1, 1) for rows in ga[1:] for block in rows]
        elif step == "w":
            kind = kinds[-1]
            groups["t"] = Group(wide, kind, *attention_weights(core, wide.back(kind), ut, gq, gk, gv))
        elif step == "p":
            kind = kinds[-2]
            groups["p"] = Group(wide, kind, *proj_weights(wide.back(kind), gat, mixed))
        elif step in ("q", "qa", "qb", "o", "oa", "ob"):
            if name == "q":
                args = ([[gq], [gk], [gv]], [w_query, w_key, w_value], NT, "norm1_grad")
            else:
                args = ([hidden], [w_down], NN, "mlp_out")
            if not paired:
                partial[name] = scattered(product(*args, False, name == "o"))
            else:
                part = product(*args, at == "b", name == "o")
                partial.setdefault(name, []).append(part if at == "b" else swapped(part))
        elif step == "in":
            input_grad, more = input_rows(here, partial["q"], frames, gh, gain1)
            sums += more
        elif step == "out":
            output, more = output_rows(
                here, partial["o"], frames, attn, output_grad, scale1, scale2
            )
            sums += more
        elif step == "sum":
            sums = add(sums, swapped(sums)) if paired else lax.psum(sums, "narrow")
        elif name == "s":
            sums = add(sums, wide.along(sums, int(at)))
    for bit in range(4, wide.bits):
        sums = add(sums, wide.along(sums, bit))
        for group in groups.values():
            group.advance()
    attention, proj = groups.pop("t"), groups.pop("p")
    gate_grad, up_grad, down_grad = finish_feed(groups.values(), counts, columns)
    query_grad, key_grad, value_grad, proj_grad = finish_attention(attention, proj)

    return (
        output,
        input_grad,
        query_grad,
        key_grad,
        value_grad,
        proj_grad.T,
        gate_grad,
        up_grad,
        down_grad.T,
        sums[4],
        sums[5],
        sums[0],
        sums[1],
        sums[2],
        sums[3],
    )


def solution(mesh):
    rows = P(("wide", "narrow"), None)
    across = P(None, "narrow")
    return jax.shard_map(
        on_device,
        mesh=mesh,
        in_specs=(rows, P("wide", None))
        + (across,) * 3
        + (P("narrow", None),)
        + (across,) * 2
        + (P("narrow", None),)
        + (P(),) * 6
        + (rows,),
        out_specs=(rows, rows)
        + (P("wide", "narrow"),) * 3
        + (P("narrow", "wide"),)
        + (P("wide", "narrow"),) * 2
        + (P("narrow", "wide"),)
        + (P(),) * 6,
        check_vma=False,
    )
```

```python
import functools
import math

import jax
import jax.numpy as jnp
import numpy as np
from jax import lax
from jax.experimental import pallas as pl
from jax.experimental.pallas import tpu as pltpu
from jax.sharding import PartitionSpec as P

HEAD_DIM = 64
HALF_WINDOW = 64
CLIPS = 6
MAX_CLIP = 384
norm_eps = 1e-05
masked_score = -1e30
COUNTS = [3, 3, 2]
KINDS = ["zy", "zx", "xyz", "xyz", "xyz"]
PLAN = [
    "F0:1", "F1:6", "F2:13", "h0:1", "ut:3", "mb:10", "a0", "turn", "p", "h1", "a1", "h2:1", "oa",
    "w", "ob", "qa:1", "h0:2", "h2", "h1:10", "ht", "h2:2", "out:2", "h1:1", "qb:1", "ht", "in",
    "h0", "hp", "e2:2", "sum", "ht:1", "hp", "s0", "s1", "e1", "s2", "hp", "e0:1", "et", "s3",
    "ep:6",
]
SHORT = ["F0", "ut", "mb", "p", "a0", "w", "h0", "hp", "ht", "q", "o", "h0", "hp", "ht", "in", "out", "sum", "s0", "s1", "s2", "s3", "h0", "hp", "ht"]
bf16 = jnp.bfloat16
f32 = jnp.float32
NN = (((1,), (0,)), ((), ()))
NT = (((1,), (1,)), ((), ()))
TN = (((0,), (0,)), ((), ()))


def dot(a, b, dims=NN):
    return lax.dot_general(a, b, dims, preferred_element_type=f32)


class Chain:
    token = None
    held = []
    weight = 0


def call(
    body,
    name,
    grid,
    in_specs,
    out_specs,
    out_shape,
    scratch=(),
    prefetch=0,
    mib=16,
    aliases=None,
    near_in=(),
    near_out=(),
):
    outputs = len(out_specs)
    before = [] if Chain.token is None else [(Chain.token, pltpu.HBM)]
    before += [(one, pltpu.VMEM) for one in Chain.held]
    Chain.held = []
    extra = len(before)
    weight, Chain.weight = 1 + Chain.weight, 0

    def inner(*refs):
        rest = refs[prefetch + extra :]
        ins = len(in_specs)
        body(*refs[:prefetch], *rest[: ins + outputs], *rest[ins + outputs + 1 :])

    anywhere = pl.BlockSpec(memory_space=pl.ANY)
    shapes = [
        (pltpu.VMEM if at in near_out else pltpu.HBM)(one.shape, one.dtype)
        for at, one in enumerate(out_shape)
    ]
    run = pl.pallas_call(
        inner,
        grid_spec=pltpu.PrefetchScalarGridSpec(
            num_scalar_prefetch=prefetch,
            grid=grid,
            in_specs=[anywhere] * extra + list(in_specs),
            out_specs=list(out_specs) + [anywhere],
            scratch_shapes=list(scratch),
        ),
        out_shape=shapes + [pltpu.HBM((8, 128), f32)],
        input_output_aliases={at + extra: out for at, out in (aliases or {}).items()},
        compiler_params=pltpu.CompilerParams(vmem_limit_bytes=mib * 2**20),
        cost_estimate=pl.CostEstimate(flops=weight, bytes_accessed=1, transcendentals=0),
        name=name,
    )

    def apply(*operands):
        placed = before + [
            (one, pltpu.VMEM if at in near_in else pltpu.HBM)
            for at, one in enumerate(operands[prefetch:])
        ]
        placed = [pltpu.with_memory_space_constraint(*one) for one in placed]
        *results, Chain.token = run(*operands[:prefetch], *placed)
        return results

    return apply


def near(shape):
    return pl.BlockSpec(memory_space=pltpu.VMEM)


def whole(shape):
    return pl.BlockSpec(
        shape, lambda *_: (0,) * len(shape), pipeline_mode=pl.Buffered(1)
    )


def like(shape, kind=bf16):
    return jax.ShapeDtypeStruct(shape, kind)


def normalise(rows):
    centred = rows - jnp.mean(rows, axis=-1, keepdims=True)
    inverse = lax.rsqrt(jnp.mean(centred * centred, axis=-1, keepdims=True) + norm_eps)
    return centred * inverse, inverse


def norm_back(incoming, unit, inverse, gain):
    scaled = incoming * gain
    return inverse * (
        scaled
        - jnp.mean(scaled, axis=-1, keepdims=True)
        - unit * jnp.mean(scaled * unit, axis=-1, keepdims=True)
    )


def rope_table():
    half = HEAD_DIM // 2
    lane = np.arange(128)
    frequency = np.exp((lane % half) * (-math.log(10000.0) / half))
    angle = np.arange(MAX_CLIP)[:, None] * frequency[None, :]
    sign = np.where(lane % HEAD_DIM < half, -1.0, 1.0)
    parts = []
    for table in (np.cos(angle), np.sin(angle) * sign):
        high = table.astype(np.float32).astype(bf16)
        parts += [high, (table - high.astype(np.float64)).astype(np.float32).astype(bf16)]
    return np.concatenate(parts, axis=1)


def swap_halves(values):
    half = HEAD_DIM // 2
    width = values.shape[-1]
    lane = lax.broadcasted_iota(jnp.int32, values.shape, 1)
    return jnp.where(
        lane % HEAD_DIM < half,
        pltpu.roll(values, width - half, 1),
        pltpu.roll(values, half, 1),
    )


def column_of(row, start, count):
    pieces = []
    for place in range(count // 128):
        piece = row[:, pl.ds(pl.multiple_of(start + place * 128, 128), 128)]
        pieces.append(jnp.broadcast_to(piece.astype(f32), (128, 128)).T)
    return jnp.concatenate(pieces, axis=0) if len(pieces) > 1 else pieces[0]


def project_body(base, *refs, parts):
    xs = refs[:parts]
    seg, gain, bias, table, wq, wk, wv, q, k, v, cos, sin, clips, kept = refs[parts:]
    step, blocks = pl.program_id(0), pl.num_programs(0)
    block = lax.rem(base[0] + step, blocks)
    rows_per = xs[0].shape[0]
    raw = xs[0][...]
    for part in range(1, parts):
        raw = jnp.where(step >= part * (blocks // parts), xs[part][...], raw)
    unit, _ = normalise(raw.astype(f32))
    normed = (unit * gain[...] + bias[...]).astype(bf16)
    kept[...] = normed
    ids = seg[...]
    mine = column_of(seg, block * rows_per, rows_per)
    clips[...] = mine
    start = jnp.zeros_like(mine)
    for clip in range(CLIPS - 1):
        count = jnp.sum((ids == clip).astype(f32), axis=-1, keepdims=True)
        start += jnp.where(mine > clip, count, 0.0)
    place = lax.broadcasted_iota(jnp.int32, mine.shape, 0) + block * rows_per
    place = place - start.astype(jnp.int32)
    lane = lax.broadcasted_iota(jnp.int32, mine.shape, 1)
    hot = jnp.concatenate(
        [(place == lane + 128 * part).astype(bf16) for part in range(MAX_CLIP // 128)], axis=1
    )
    rows = dot(hot, table[...])
    cosine = rows[:, :128] + rows[:, 128:256]
    sine = rows[:, 256:384] + rows[:, 384:]
    cos[...] = cosine
    sin[...] = sine
    for weights, out, factor in ((wq, q, HEAD_DIM**-0.5), (wk, k, 1.0)):
        flat = dot(normed, weights[...])
        for at in range(0, flat.shape[1], 128):
            part = flat[:, at : at + 128]
            part = part * cosine + swap_halves(part) * sine
            out[:, at : at + 128] = (part * factor).astype(bf16)
    v[...] = dot(normed, wv[...]).astype(bf16)


def project(base, xs, seg, gain, bias, wq, wk, wv, rows_per=256):
    parts = len(xs)
    each, width = xs[0].shape
    length = parts * each
    heads = wq.shape[1]
    blocks = length // rows_per

    def out(columns):
        return pl.BlockSpec((rows_per, columns), lambda i, base: (lax.rem(base[0] + i, blocks), 0))

    def piece(part):
        count = each // rows_per
        return pl.BlockSpec(
            (rows_per, width), lambda i, base: (jnp.clip(i - part * count, 0, count - 1), 0)
        )

    table = rope_table()
    return call(
        functools.partial(project_body, parts=parts),
        "project",
        (blocks,),
        [piece(part) for part in range(parts)]
        + [
            whole(seg.shape),
            whole((1, width)),
            whole((1, width)),
            whole(table.shape),
            whole(wq.shape),
            whole(wk.shape),
            whole(wv.shape),
        ],
        [out(heads)] * 3
        + [out(128)] * 3
        + [pl.BlockSpec((rows_per, width), lambda i, base: (i, 0))],
        [like((length, heads))] * 3 + [like((length, 128), f32)] * 3 + [like((length, width))],
        prefetch=1,
        near_out=[0, 1, 2, 5],
    )(base, *xs, seg, gain, bias, jnp.asarray(table), wq, wk, wv)


def band(block, rows_per, span, length):
    first = block * rows_per
    start = jnp.clip(first - HALF_WINDOW, 0, length - span)
    return first, pl.multiple_of(start, HALF_WINDOW)


def two_heads(values):
    lane = lax.broadcasted_iota(jnp.int32, values.shape, 1)
    zero = jnp.zeros_like(values)
    return jnp.concatenate(
        [jnp.where(lane < HEAD_DIM, values, zero), jnp.where(lane < HEAD_DIM, zero, values)], axis=0
    )


def one_each(stacked):
    count = stacked.shape[0] // 2
    lane = lax.broadcasted_iota(jnp.int32, (count, 128), 1)
    return jnp.where(lane < HEAD_DIM, stacked[:count], stacked[count:])


def attend_body(base, q, k, v, seg, clips, *refs, span):
    o, weights = refs[-2:]
    rows_per = q.shape[0]
    length = k.shape[0]
    block = base[0] + pl.program_id(0)
    first, start = band(block, rows_per, span, length)
    mine = seg[:, pl.ds(first, rows_per)]
    theirs = clips[pl.ds(start, span), :]
    gap = (
        lax.broadcasted_iota(jnp.int32, (span, rows_per), 0)
        - lax.broadcasted_iota(jnp.int32, (span, rows_per), 1)
        + (start - first)
    )
    allowed = (gap >= -HALF_WINDOW) & (gap < HALF_WINDOW) & (theirs == mine.astype(f32))
    penalty = jnp.where(allowed, 0.0, masked_score)
    penalty = jnp.concatenate([penalty, penalty], axis=1)
    for pair in range(q.shape[1] // 128):
        lanes = slice(pair * 128, pair * 128 + 128)
        keys = k[pl.ds(start, span), lanes]
        values = v[pl.ds(start, span), lanes]
        scores = dot(keys, two_heads(q[:, lanes]), NT) + penalty
        lifted = jnp.exp(scores - jnp.max(scores, axis=0, keepdims=True))
        chances = (lifted * (1.0 / jnp.sum(lifted, axis=0, keepdims=True))).astype(bf16)
        weights[0, pair] = chances
        o[:, lanes] = one_each(dot(chances, values, TN)).astype(bf16)


def attend(base, q, k, v, seg, clips, blocks, rows_per, span, weights=None):
    length, heads = q.shape
    pairs = heads // 128
    kept = [] if weights is None else [weights]
    return call(
        functools.partial(attend_body, span=span),
        "attend",
        (blocks,),
        [
            pl.BlockSpec((rows_per, heads), lambda i, base: (base[0] + i, 0)),
            near(k.shape),
            near(v.shape),
            whole(seg.shape),
            near(clips.shape),
        ]
        + [pl.BlockSpec(memory_space=pl.ANY)] * len(kept),
        [
            pl.BlockSpec((rows_per, heads), lambda i, base: (i, 0)),
            pl.BlockSpec((1, pairs, span, 2 * rows_per), lambda i, base: (base[0] + i, 0, 0, 0)),
        ],
        [like((blocks * rows_per, heads)), like((length // rows_per, pairs, span, 2 * rows_per))],
        prefetch=1,
        aliases={6: 1} if kept else None,
        near_in=[0, 1, 2, 4],
    )(base, q, k, v, seg, clips, *kept)


def attend_back_body(base, *refs, parts, span, start, last):
    ga, wo, q, k, v, weights, cos, sin, *refs = refs[:parts], *refs[parts:]
    gq, gk, gv, acc_k, acc_v = refs[-5:]
    rows_per = q.shape[0]
    length = k.shape[0]
    block = base[0] + pl.program_id(0)
    _, first = band(block, rows_per, span, length)

    if start:

        @pl.when(pl.program_id(0) == 0)
        def _():
            acc_k[...] = jnp.zeros_like(acc_k)
            acc_v[...] = jnp.zeros_like(acc_v)

    rows = ga[0][...]
    for part in range(1, parts):
        rows = jnp.where(pl.program_id(0) >= part * (pl.num_programs(0) // parts), ga[part][...], rows)
    go = dot(rows, wo[...], NT).astype(bf16)
    mine = pl.ds(pl.multiple_of(block * rows_per, rows_per), rows_per)
    cosine, sine = cos[mine, :], sin[mine, :]
    keys_at = pl.ds(first, span)
    for pair in range(q.shape[1] // 128):
        lanes = slice(pair * 128, pair * 128 + 128)
        keys = k[keys_at, lanes]
        values = v[keys_at, lanes]
        chances = weights[0, pair]
        full = chances.astype(f32)
        go_two = two_heads(go[:, lanes])
        change = dot(values, go_two, NT)
        weighted = jnp.sum(full * change, axis=0, keepdims=True)
        gs = (full * (change - weighted)).astype(bf16)
        gq_rows = one_each(dot(gs, keys, TN)) * HEAD_DIM**-0.5
        gq[:, lanes] = (gq_rows * cosine - swap_halves(gq_rows) * sine).astype(bf16)
        acc_k[keys_at, lanes] += dot(gs, two_heads(q[:, lanes]))
        acc_v[keys_at, lanes] += dot(chances, go_two)

    if last:

        @pl.when(pl.program_id(0) == pl.num_programs(0) - 1)
        def _():
            @pl.loop(0, length // rows_per)
            def _(at):
                here = pl.ds(pl.multiple_of(at * rows_per, rows_per), rows_per)
                gv[here, :] = acc_v[here, :].astype(bf16)
                for pair in range(q.shape[1] // 128):
                    lanes = slice(pair * 128, pair * 128 + 128)
                    rows = acc_k[here, lanes]
                    rows = rows * cos[here, :] - swap_halves(rows) * sin[here, :]
                    gk[here, lanes] = rows.astype(bf16)


def attend_back(base, ga, wo, q, k, v, weights, cos, sin, rows_per, span, kept, last):
    length, heads = q.shape
    pairs = heads // 128
    parts = len(ga)
    each, width = ga[0].shape
    rows = parts * each
    row = pl.BlockSpec((rows_per, heads), lambda i, base: (base[0] + i, 0))
    full = near((length, heads))

    def block(part):
        count = each // rows_per
        return pl.BlockSpec(
            (rows_per, width), lambda i, base: (jnp.clip(i - part * count, 0, count - 1), 0)
        )

    return call(
        functools.partial(
            attend_back_body, parts=parts, span=span, start=not kept, last=last
        ),
        "attend_back",
        (rows // rows_per,),
        [block(part) for part in range(parts)]
        + [
            whole(wo.shape),
            row,
            full,
            full,
            pl.BlockSpec((1, pairs, span, 2 * rows_per), lambda i, base: (base[0] + i, 0, 0, 0)),
            whole(cos.shape),
            whole(sin.shape),
        ]
        + [full if at > 0 else pl.BlockSpec(memory_space=pl.ANY) for at in range(len(kept))],
        [row, full, full, full, full],
        [like((length, heads))] * 3 + [like((length, heads), f32)] * 2,
        prefetch=1,
        aliases={8 + parts + at: at for at in range(len(kept))},
        near_in=list(range(parts))
        + [parts + at for at in (1, 2, 3)]
        + [parts + 7 + at for at in range(len(kept))],
        near_out=range(5),
    )(base, *ga, wo, q, k, v, weights, cos, sin, *kept)


def put_transposed(target, values):
    for at in range(0, values.shape[1], 128):
        target[at : at + 128, :] = values[:, at : at + 128].T


def cotangent_body(dy, scale, gm, gmt):
    scaled = (dy[...].astype(f32) * scale[...]).astype(bf16)
    gm[...] = scaled
    put_transposed(gmt, scaled)


def cotangent(dy, scale, near_in=0, rows_per=256):
    rows, width = dy.shape
    row = pl.BlockSpec((rows_per, width), lambda i: (i, 0))
    return call(
        cotangent_body,
        "cotangent",
        (rows // rows_per,),
        [row, whole((1, width))],
        [row, pl.BlockSpec((width, rows_per), lambda i: (0, i))],
        [like((rows, width)), like((width, rows))],
        near_in=range(near_in),
        near_out=range(2 * near_in),
    )(dy, scale)


def place_body(received, own, own_turned, turned, *copies):
    put_transposed(turned, received[...])
    for copy, values in zip(copies, (received, own, own_turned)):
        copy[...] = values[...]


def place(received, own, own_turned, rows_per=256):
    length, width = received.shape
    row = pl.BlockSpec((rows_per, width), lambda i: (i, 0))
    column = pl.BlockSpec((width, rows_per), lambda i: (0, i))
    return call(
        place_body,
        "place",
        (length // rows_per,),
        [row, row, column],
        [column, row, row, column],
        [like((width, length)), like((length, width)), like((length, width)), like((width, length))],
        near_in=range(1),
        near_out=range(4),
    )(received, own, own_turned)


def turn_body(values, out):
    put_transposed(out, values[...])


def turn(values, near_in=0, near_out=0, start=0, length=None, rows_per=256):
    width = values.shape[1]
    length = length or values.shape[0]
    rows_per = min(rows_per, length)
    first = start // rows_per
    return call(
        turn_body,
        "turn",
        (length // rows_per,),
        [pl.BlockSpec((rows_per, width), lambda i: (i + first, 0))],
        [pl.BlockSpec((width, rows_per), lambda i: (0, i))],
        [like((width, length))],
        near_in=range(near_in),
        near_out=range(near_out),
    )(values)[0]


def middle_body(*refs, parts):
    mixed = refs[: 2 * parts]
    x, scale, gain, bias = refs[2 * parts : 2 * parts + 4]
    attn, m, mt, *sent = refs[2 * parts + 4 :]
    total = dot(mixed[0][...], mixed[1][...])
    for part in range(1, parts):
        total += dot(mixed[2 * part][...], mixed[2 * part + 1][...])
    low = total.astype(bf16)
    attn[...] = low
    rows = x[...].astype(f32) + scale[...] * low.astype(f32)
    unit, _ = normalise(rows)
    normed = (unit * gain[...] + bias[...]).astype(bf16)
    m[...] = normed
    put_transposed(mt, normed)
    for copy in sent:
        copy[...] = normed


def middle(mixed, x, scale, gain, bias, sent, rows_per=256):
    rows, width = x.shape
    specs, operands = [], []
    for left, right in mixed:
        specs += [
            pl.BlockSpec((rows_per, left.shape[1]), lambda i: (i, 0)),
            whole(right.shape),
        ]
        operands += [left, right]
    row = pl.BlockSpec((rows_per, width), lambda i: (i, 0))
    return call(
        functools.partial(middle_body, parts=len(mixed)),
        "middle",
        (rows // rows_per,),
        specs + [row, whole((1, width)), whole((1, width)), whole((1, width))],
        [row, row, pl.BlockSpec((width, rows_per), lambda i: (0, i))] + [row] * sent,
        [like((rows, width)), like((rows, width)), like((width, rows))]
        + [like((rows, width))] * sent,
        near_in=[2, 3] * (len(mixed) > 1),
    )(*operands, x, scale, gain, bias)


def gathered(source, back, quarter, piece):
    groups = source.shape[0] // (4 * piece)
    return jnp.concatenate(
        [
            source[pl.ds(pl.multiple_of(back[quarter * groups + at] * piece, piece), piece), :]
            for at in range(groups)
        ],
        axis=0,
    )


def put_quarter(sent, kept, quarter, start, values):
    height = values.shape[0]
    place = slice((quarter % 2) * height, (quarter % 2) * height + height)
    (sent if quarter < 2 else kept)[place, start : start + values.shape[1]] = values


def feed_grads_body(back, *refs, parts):
    mt, gmt = refs[:parts], refs[parts : 2 * parts]
    hid, gg, gu, sent, kept = refs[2 * parts :]
    piece = gmt[0].shape[0] // back.shape[0]
    columns = hid.shape[1]
    each = gmt[0].shape[1]

    def product(lefts, right):
        total = dot(lefts[0], right[:each, :])
        for part in range(1, parts):
            total += dot(lefts[part], right[part * each : part * each + each, :])
        return total.astype(bf16)

    for quarter in range(4):
        grad_rows = [gathered(source, back, quarter, piece) for source in gmt]
        put_quarter(sent, kept, quarter, 0, product(grad_rows, hid))
        rows = [gathered(source, back, quarter, piece) for source in mt]
        put_quarter(sent, kept, quarter, columns, product(rows, gg))
        put_quarter(sent, kept, quarter, 2 * columns, product(rows, gu))


def feed_acts_body(m, gm, wg, wu, wd, hid, gg, gu, total, fresh, rows_per):
    each = m[0].shape[0]
    for part in range(len(m)):

        @pl.loop(0, each // rows_per)
        def _(at, part=part):
            here = pl.ds(pl.multiple_of(at * rows_per, rows_per), rows_per)
            there = pl.ds(pl.multiple_of(part * each + at * rows_per, rows_per), rows_per)
            rows = m[part][here, :]
            gate = dot(rows, wg[...])
            up = dot(rows, wu[...])
            back = dot(gm[part][here, :], wd[...], NT)
            sigma = 1.0 / (1.0 + jnp.exp(-gate))
            active = gate * sigma
            hid[there, :] = (active * up).astype(bf16)
            gate_back = (back * up * sigma * (1.0 + gate * (1.0 - sigma))).astype(bf16)
            up_back = (back * active).astype(bf16)
            gg[there, :] = gate_back
            gu[there, :] = up_back
            both = jnp.concatenate([gate_back, up_back], axis=1)
            for start in range(0, total.shape[1], 256):
                cols = slice(start, start + 256)
                weights = jnp.concatenate([wg[cols, :], wu[cols, :]], axis=1)
                more = dot(both, weights, NT)
                total[there, cols] = jnp.where(fresh, more, total[there, cols] + more)


def feed_body(back, *refs, parts, rows_per, first, sent_blocks):
    m, gm, mt, gmt = (refs[at * parts : (at + 1) * parts] for at in range(4))
    wg, wu, wd, *refs = refs[4 * parts :]
    gg, gu = refs[-2:]
    hid, sent, kept, total, *blocks = refs[-6 - sent_blocks : -2]
    step = pl.program_id(0)
    if first:
        start = step == 0
    else:
        start = step < 0

    feed_acts_body(m, gm, wg, wu, wd, hid, gg, gu, total, start, rows_per)
    feed_grads_body(back, *mt, *gmt, hid, gg, gu, sent, kept, parts=parts)
    if blocks:

        @pl.when(step == pl.num_programs(0) - 1)
        def _():
            height = blocks[0].shape[0]
            base = total.shape[0] // 2
            for at, out in enumerate(blocks):
                out[...] = total[base + at * height : base + at * height + height, :].astype(bf16)


def feed(back, m, gm, mt, gmt, wg, wu, wd, first, count, columns, total, sent_blocks, rows_per=512):
    each, width = gm[0].shape
    parts = len(gm)
    length = each * parts
    col = pl.BlockSpec((width, columns), lambda j, back: (0, j + first))
    out = pl.BlockSpec((length, columns), lambda j, back: (0, j))
    grad = pl.BlockSpec((width // 2, 3 * columns), lambda j, back: (0, j))
    so_far = [] if total is None else [total]
    block = (length // 2 // max(sent_blocks, 1), width)
    return call(
        functools.partial(
            feed_body, parts=parts, rows_per=rows_per, first=total is None, sent_blocks=sent_blocks
        ),
        "feed",
        (count,),
        [near((each, width))] * (4 * parts)
        + [col, col, pl.BlockSpec((columns, width), lambda j, back: (j + first, 0))]
        + [near((length, width))] * len(so_far),
        [out] + [grad] * 2 + [near((length, width))] + [whole(block)] * sent_blocks,
        [like((length, columns * count))]
        + [like((width // 2, 3 * columns * count))] * 2
        + [like((length, width), f32)]
        + [like(block)] * sent_blocks,
        scratch=[pltpu.VMEM((length, columns), bf16)] * 2,
        prefetch=1,
        near_in=list(range(4 * parts)) + [4 * parts + 3] * len(so_far),
        near_out=range(1, 4 + sent_blocks),
        aliases={4 * parts + 4: 3} if so_far else None,
        mib=24,
    )(back, *m, *gm, *mt, *gmt, wg, wu, wd, *so_far)


def multiply_body(base, *refs, counts, dims):
    lefts, rights = refs[: sum(counts)], refs[sum(counts) : sum(counts) + len(counts)]
    outs = refs[sum(counts) + len(counts) :]
    total = None
    piece = 0
    for count, right in zip(counts, rights):
        at = 0
        for left in lefts[piece : piece + count]:
            depth = left.shape[1]
            if dims is NN:
                part = dot(left[...], right[at : at + depth, :])
            else:
                part = dot(left[...], right[:, at : at + depth], NT)
            total = part if total is None else total + part
            at += depth
        piece += count
    total = total.astype(outs[0].dtype)
    if len(outs) == 1:
        outs[0][...] = total
        return
    for block, out in enumerate(outs):

        @pl.when(pl.program_id(0) == block)
        def _(out=out):
            out[...] = total


def multiply(base, rows, lefts, rights, dims, name, kind=bf16, rows_per=256, near_in=(), near_out=(), apart=False):
    width = rights[0].shape[1 if dims is NN else 0]
    pieces = [piece for left in lefts for piece in left]
    return call(
        functools.partial(multiply_body, counts=[len(left) for left in lefts], dims=dims),
        name,
        (rows // rows_per,),
        [
            pl.BlockSpec((rows_per, piece.shape[1]), lambda i, base: (base[0] + i, 0))
            for piece in pieces
        ]
        + [whole(right.shape) for right in rights],
        [whole((rows_per, width))] * (rows // rows_per)
        if apart
        else [pl.BlockSpec((rows_per, width), lambda i, base: (i, 0))],
        [like((rows_per, width), kind)] * (rows // rows_per)
        if apart
        else [like((rows, width), kind)],
        prefetch=1,
        mib=24,
        near_in=near_in,
        near_out=near_out,
    )(base, *pieces, *rights)


def middle_back_body(*refs, parts):
    pieces = sum(parts)
    x, attn, dy, scale, gain, gh, ga, gat, sums, *sent = refs[pieces:]
    step = pl.program_id(0)
    incoming = None
    at = 0
    for count in parts:
        rows = refs[at][...].astype(f32)
        for block in range(1, count):
            rows = jnp.where(step == block, refs[at + block][...].astype(f32), rows)
        incoming = rows if incoming is None else incoming + rows
        at += count
    attn_rows = attn[...].astype(f32)
    unit, inverse = normalise(x[...].astype(f32) + scale[...] * attn_rows)
    grad = dy[...].astype(f32) + norm_back(incoming, unit, inverse, gain[...])
    gh[...] = grad
    low = (scale[...] * grad).astype(bf16)
    ga[...] = low
    for block, out in enumerate(sent):

        @pl.when(step == block)
        def _(out=out):
            out[...] = low

    put_transposed(gat, low)

    @pl.when(step == 0)
    def _():
        sums[...] = jnp.zeros_like(sums)

    sums[0:1, :] += jnp.sum(incoming * unit, axis=0, keepdims=True)
    sums[1:2, :] += jnp.sum(incoming, axis=0, keepdims=True)
    sums[2:3, :] += jnp.sum(attn_rows * grad, axis=0, keepdims=True)


def middle_back(partial, x, attn, dy, scale, gain, sent, rows_per=256):
    rows, width = x.shape
    blocks = rows // rows_per
    row = pl.BlockSpec((rows_per, width), lambda i: (i, 0))
    partial = [part if isinstance(part, list) else [part] for part in partial]
    specs = [
        row if len(part) == 1 else whole((rows_per, width)) for part in partial for _ in part
    ]
    flat = [block for part in partial for block in part]
    return call(
        functools.partial(middle_back_body, parts=[len(part) for part in partial]),
        "middle_back",
        (blocks,),
        specs + [row, row, row, whole((1, width)), whole((1, width))],
        [
            row,
            row,
            pl.BlockSpec((width, rows_per), lambda i: (0, i)),
            whole((8, width)),
        ]
        + [whole((rows_per, width))] * (blocks * sent),
        [
            like((rows, width), f32),
            like((rows, width)),
            like((width, rows)),
            like((8, width), f32),
        ]
        + [like((rows_per, width))] * (blocks * sent),
        near_in=range(len(flat)),
        near_out=[1, 2] + list(range(4, 4 + blocks * sent)),
    )(*flat, x, attn, dy, scale, gain)


def weights_body(core, back, *refs, parts):
    ut, gq, gk, gv, sent, kept = refs
    piece = ut.shape[0] // back.shape[0]
    each = ut.shape[1] // parts
    heads = gq.shape[1]

    def product(lefts, right):
        total = None
        for part in range(parts):
            first = (core[0] if part == 0 else 1 - core[0]) * each if parts == 2 else 0
            there = pl.ds(pl.multiple_of(first, each), each) if parts == 2 else slice(None)
            one = dot(lefts[part], right[there, :])
            total = one if total is None else total + one
        return total.astype(bf16)

    for quarter in range(4):
        whole_rows = gathered(ut, back, quarter, piece)
        rows = [whole_rows[:, part * each : part * each + each] for part in range(parts)]
        for place, right in enumerate((gq, gk, gv)):
            put_quarter(sent, kept, quarter, place * heads, product(rows, right))


def attention_weights(core, back, ut, gq, gk, gv, parts):
    width = ut.shape[0]
    shape = (width // 2, 3 * gq.shape[1])
    operands = (ut, gq, gk, gv)
    close = range(1, 4)
    return call(
        functools.partial(weights_body, parts=parts),
        "attention_weights",
        (1,),
        [(near if at in close else whole)(one.shape) for at, one in enumerate(operands)],
        [near(shape)] * 2,
        [like(shape)] * 2,
        prefetch=2,
        near_in=close,
        near_out=range(2),
    )(core, back, *operands)


def proj_body(back, *refs, parts, blocks):
    gat, o, (sent, kept) = refs[:blocks], refs[blocks : blocks + parts], refs[blocks + parts :]
    piece = gat[0].shape[0] // back.shape[0]
    each = o[0].shape[0]
    for quarter in range(4):
        proj = None
        at = 0
        for block in gat:
            size = block.shape[1]
            right = o[at // each][at % each : at % each + size, :]
            one = dot(gathered(block, back, quarter, piece), right)
            proj = one if proj is None else proj + one
            at += size
        put_quarter(sent, kept, quarter, 0, proj.astype(bf16))


def proj_weights(back, gat, o):
    shape = (gat[0].shape[0] // 2, o[0].shape[1])
    parts, blocks = len(o), len(gat)
    return call(
        functools.partial(proj_body, parts=parts, blocks=blocks),
        "proj_weights",
        (1,),
        [near(one.shape) for one in gat] + [whole(one.shape) for one in o],
        [near(shape)] * 2,
        [like(shape)] * 2,
        prefetch=1,
        near_in=range(blocks),
        near_out=range(2),
    )(back, *gat, *o)


def output_body(core, *refs, parts):
    partial = refs[:parts]
    x, attn, dy, scale_attn, scale_mlp, out, sums = refs[parts:]
    total = partial[0][...].astype(f32)
    for part in range(1, parts):
        total += partial[part][...].astype(f32)
    middle_rows = x[...].astype(f32) + scale_attn[...] * attn[...].astype(f32)
    out[...] = (middle_rows + scale_mlp[...] * total).astype(bf16)

    @pl.when(pl.program_id(0) == 0)
    def _():
        sums[...] = jnp.zeros_like(sums)

    sums[3:4, :] += jnp.sum(total * dy[...].astype(f32), axis=0, keepdims=True)


def output_rows(core, partial, x, attn, dy, scale_attn, scale_mlp, rows_per=256):
    rows, width = x.shape
    rows_per = min(rows_per, rows)
    row = pl.BlockSpec((rows_per, width), lambda i, core: (i, 0))
    own = pl.BlockSpec((rows_per, width), lambda i, core: (i + core[0], 0))
    return call(
        functools.partial(output_body, parts=len(partial)),
        "output_rows",
        (rows // rows_per,),
        [row] * len(partial) + [row, own, row] + [whole((1, width))] * 2,
        [row, whole((8, width))],
        [like((rows, width)), like((8, width), f32)],
        prefetch=1,
        near_in=range(len(partial)),
    )(core, *partial, x, attn, dy, scale_attn, scale_mlp)


def input_body(core, *refs, parts):
    partial = refs[:parts]
    x, gh, gain, out, sums = refs[parts:]
    incoming = partial[0][...].astype(f32)
    for part in range(1, parts):
        incoming += partial[part][...].astype(f32)
    unit, inverse = normalise(x[...].astype(f32))
    out[...] = (gh[...] + norm_back(incoming, unit, inverse, gain[...])).astype(bf16)

    @pl.when(pl.program_id(0) == 0)
    def _():
        sums[...] = jnp.zeros_like(sums)

    sums[4:5, :] += jnp.sum(incoming * unit, axis=0, keepdims=True)
    sums[5:6, :] += jnp.sum(incoming, axis=0, keepdims=True)


def input_rows(core, partial, x, gh, gain, rows_per=256):
    rows, width = x.shape
    rows_per = min(rows_per, rows)
    row = pl.BlockSpec((rows_per, width), lambda i, core: (i, 0))
    own = pl.BlockSpec((rows_per, width), lambda i, core: (i + core[0], 0))
    return call(
        functools.partial(input_body, parts=len(partial)),
        "input_rows",
        (rows // rows_per,),
        [row] * len(partial) + [row, own] + [whole((1, width))],
        [row, whole((8, width))],
        [like((rows, width)), like((8, width), f32)],
        prefetch=1,
        near_in=range(len(partial)),
    )(core, *partial, x, gh, gain)


class Wide:
    def __init__(self):
        self.size = lax.axis_size("wide")
        self.bits = self.size.bit_length() - 1
        assert self.size == 1 << self.bits and self.bits > 2
        self.place = lax.axis_index("wide").astype(jnp.int32)
        self.cores = lax.axis_size("narrow")
        self.core = lax.axis_index("narrow")

    def orders(self, kind):
        rest = list(range(2, self.bits))
        near_far, far_near = [0, 1] + rest, [1, 0] + rest
        return {
            "xyz": (near_far, far_near),
            "zy": (near_far, rest + [1, 0]),
            "zx": (rest + [0, 1], far_near),
            "mid": ([0] + rest + [1], [1] + rest + [0]),
        }[kind]

    def back(self, kind):
        found = []
        for order in self.orders(kind):
            groups = []
            for place in range(self.size):
                apart = 0
                for step, bit in enumerate(order):
                    apart |= (1 - ((place >> (self.bits - 1 - step)) & 1)) << bit
                groups.append(apart)
            found.append(jnp.array(groups, jnp.int32))
        return self.place ^ jnp.where(self.core % 2 == 0, *found)

    def hop(self, values, kind, step):
        orders = self.orders(kind)
        pairs = []
        for group in range(self.size):
            for core in range(self.cores):
                target = group ^ (1 << orders[core % 2][step])
                pairs.append((group * self.cores + core, target * self.cores + core))
        return lax.ppermute(values, ("wide", "narrow"), pairs)

    def along(self, values, bit):
        return lax.ppermute(values, "wide", [(i, i ^ (1 << bit)) for i in range(self.size)])


class Group:
    def __init__(self, wide, kind, sent, kept):
        self.wide, self.kind, self.step = wide, kind, 0
        self.kept, self.got = kept, wide.hop(sent, kind, 0)

    def advance(self):
        sent, self.kept = add_again(self.kept, self.got)
        self.step += 1
        self.got = self.wide.hop(sent, self.kind, self.step)


def add_body(left, right, out):
    out[...] = left[...] + right[...]


def add(left, right):
    return call(
        add_body,
        "add",
        (),
        [near(left.shape)] * 2,
        [near(left.shape)],
        [like(left.shape, left.dtype)],
        near_in=range(2),
        near_out=range(1),
    )(left, right)[0]


def add_again_body(keep, got, sent, rest):
    half = sent.shape[0]
    sent[...] = keep[:half, :] + got[:half, :]
    rest[...] = keep[half:, :] + got[half:, :]


def add_again(keep, got):
    shape = (keep.shape[0] // 2, keep.shape[1])
    return call(
        add_again_body,
        "add_again",
        (),
        [near(keep.shape)] * 2,
        [near(shape)] * 2,
        [like(shape)] * 2,
        near_in=range(2),
        near_out=range(2),
    )(keep, got)


def finish_feed_body(*refs, counts, columns):
    gate, up, down = refs[-3:]
    at = 0
    for group, count in enumerate(counts):
        kept, got = refs[2 * group : 2 * group + 2]
        for block in range(count):
            for part, out in enumerate((down, gate, up)):
                there = slice((3 * block + part) * columns, (3 * block + part + 1) * columns)
                out[:, at : at + columns] = kept[:, there].astype(f32) + got[:, there].astype(f32)
            at += columns


def finish_feed(groups, counts, columns):
    operands = [part for group in groups for part in (group.kept, group.got)]
    shape = (operands[0].shape[0], sum(counts) * columns)
    return call(
        functools.partial(finish_feed_body, counts=counts, columns=columns),
        "finish_feed",
        (1,),
        [near(part.shape) for part in operands],
        [whole(shape)] * 3,
        [like(shape, f32)] * 3,
        near_in=range(len(operands)),
    )(*operands)


def finish_attention_body(kept, got, proj_kept, proj_got, *outs):
    heads = outs[0].shape[1]
    outs[3][...] = proj_kept[...].astype(f32) + proj_got[...].astype(f32)
    for place, out in enumerate(outs[:3]):
        there = slice(place * heads, place * heads + heads)
        out[...] = kept[:, there].astype(f32) + got[:, there].astype(f32)


def finish_attention(group, proj):
    operands = (group.kept, group.got, proj.kept, proj.got)
    return call(
        finish_attention_body,
        "finish_attention",
        (1,),
        [near(one.shape) for one in operands],
        [whole(proj.kept.shape)] * 4,
        [like(proj.kept.shape, f32)] * 4,
        near_in=range(4),
    )(*operands)


def on_device(
    frames,
    segment_ids,
    w_query,
    w_key,
    w_value,
    w_out,
    w_gate,
    w_up,
    w_down,
    norm1_gain,
    norm1_bias,
    norm2_gain,
    norm2_bias,
    scale_attn,
    scale_mlp,
    output_grad,
):
    Chain.token, Chain.held, Chain.weight = None, [], 0
    paired = lax.axis_size("narrow") == 2
    narrow = lax.axis_index("narrow").astype(jnp.int32)
    wide = Wide()
    rows_own, width = frames.shape
    length = segment_ids.shape[1]
    units = w_gate.shape[1]
    row = lambda vector: vector.reshape(1, -1)
    gain1, bias1, gain2, bias2 = map(row, (norm1_gain, norm1_bias, norm2_gain, norm2_bias))
    scale1, scale2 = row(scale_attn), row(scale_mlp)
    rows_per, span = 128, 128 + 2 * HALF_WINDOW
    core = (narrow if paired else narrow * 0).reshape(1)
    rows_done = length // 2 if paired else length

    def swapped(values):
        return lax.ppermute(values, "narrow", [(0, 1), (1, 0)])

    def both(values):
        return (values, swapped(values)) if paired else (values,)

    def bases(size):
        if paired:
            return [(1 - core) * (rows_done // size), core * (rows_done // size)]
        return [core]

    if paired:
        frame_rows, grad_rows, w_out_all = both(frames), both(output_grad), both(w_out)
    else:
        frame_rows = (lax.all_gather(frames, "narrow", axis=0, tiled=True),)
        grad_rows = (lax.all_gather(output_grad, "narrow", axis=0, tiled=True),)
        w_out_all = (lax.all_gather(w_out, "narrow", axis=0, tiled=True),)
    x, dy = frame_rows[0], grad_rows[0]
    scaled = [cotangent(dy, scale2)]
    q, k, v, cos, sin, clips, normed = project(
        bases(256)[-1], frame_rows, segment_ids, gain1, bias1, w_query, w_key, w_value
    )
    mixed, chances = [], None
    for base in bases(rows_per):
        o_part, chances = attend(
            base, q, k, v, segment_ids, clips, rows_done // rows_per, rows_per, span, chances
        )
        mixed.insert(0, o_part)
    if paired:
        o_all = (mixed[0], swapped(mixed[1]))
    else:
        o_all = (lax.all_gather(mixed[0], "narrow", axis=1, tiled=True),)
    attn, m, mt, *sent = middle(list(zip(o_all, w_out_all)), x, scale1, gain2, bias2, paired)
    m, mt = (m,), (mt,)
    for block in sent:
        received = swapped(block)
        scaled.append(cotangent(grad_rows[1], scale2, 1))
        turned, *copies = place(received, m[0], mt[0])
        m, mt = (copies[1], copies[0]), (copies[2], turned)
    gm, gmt = zip(*scaled)

    def product(lefts, rights, dims, name, own, relative, apart=False):
        if not paired:
            return multiply(core, length, lefts, rights, dims, name, f32)[0]
        other, mine = [core * 0 + rows_done // 256, core * 0] if relative else bases(256)
        place = mine if own else other
        results = multiply(
            place, rows_done, lefts, rights, dims, name, near_out=range(4), apart=apart
        )
        return results if apart else results[0]

    def scattered(part):
        return [lax.psum_scatter(part, "narrow", scatter_dimension=0, tiled=True)]

    columns = min(256, units)
    total = units // columns
    counts, kinds, plan = (COUNTS, KINDS, PLAN) if total == sum(COUNTS) else ([total], ["xyz"] * 3, SHORT)
    here = (narrow * 0 if paired else narrow * (rows_own // min(256, rows_own))).reshape(1)
    groups, hidden, grads, partial, norm2 = {}, [], (), {}, None

    for entry in plan:
        step, _, weight = entry.partition(":")
        Chain.weight += int(weight or 0) * 1150000000
        name, at = step[0], step[1:]
        if name == "F":
            at = int(at)
            where = (w_gate, w_up, w_down, sum(counts[:at]), counts[at], columns)
            sent = 2 if paired and at == len(counts) - 1 else 0
            outs = feed(wide.back(kinds[at]), m, gm, mt, gmt, *where, norm2, sent)
            hidden.append(outs[0])
            groups[str(at)] = Group(wide, kinds[at], *outs[1:3])
            norm2 = outs[3]
            norm2_sent = outs[4:]
            if at == len(counts) - 1 and paired:
                norm2_sent = [swapped(block) for block in norm2_sent]
        elif name == "h":
            groups[at].advance()
        elif name == "e":
            Chain.held = [*Chain.held, groups[at].got]
        elif step == "mb":
            norm2 = [norm2, norm2_sent] if paired else [lax.psum(norm2, "narrow")]
            gh, ga, gat, sums, *sent = middle_back(norm2, x, attn, dy, scale1, gain2, paired)
            if not paired:
                sums = jnp.where(narrow == 0, sums, 0.0)
            ga = [[ga]] + [[swapped(block) for block in sent]] * paired
            gat = [gat]
        elif name == "a":
            at = int(at)
            base = bases(rows_per)[-1 - at]
            last = at == len(ga) - 1
            grads = attend_back(
                base, ga[at], w_out, q, k, v, chances, cos, sin, rows_per, span, grads, last
            )
            gq, gk, gv = grads[:3]
        elif step == "ut":
            ut = turn(normed)
        elif step == "turn":
            gat += [turn(block, 1, 1) for rows in ga[1:] for block in rows]
        elif step == "w":
            kind = kinds[-1]
            groups["t"] = Group(wide, kind, *attention_weights(core, wide.back(kind), ut, gq, gk, gv, 1 + paired))
        elif step == "p":
            kind = kinds[-2]
            groups["p"] = Group(wide, kind, *proj_weights(wide.back(kind), gat, mixed))
        elif step in ("q", "qa", "qb", "o", "oa", "ob"):
            if name == "q":
                args = ([[gq], [gk], [gv]], [w_query, w_key, w_value], NT, "norm1_grad")
            else:
                args = ([hidden], [w_down], NN, "mlp_out")
            if not paired:
                partial[name] = scattered(product(*args, False, name == "o"))
            else:
                part = product(*args, at == "b", name == "o")
                partial.setdefault(name, []).append(part if at == "b" else swapped(part))
        elif step == "in":
            input_grad, more = input_rows(here, partial["q"], frames, gh, gain1)
            sums += more
        elif step == "out":
            output, more = output_rows(
                here, partial["o"], frames, attn, output_grad, scale1, scale2
            )
            sums += more
        elif step == "sum":
            sums = add(sums, swapped(sums)) if paired else lax.psum(sums, "narrow")
        elif name == "s":
            sums = add(sums, wide.along(sums, int(at)))
    for bit in range(4, wide.bits):
        sums = add(sums, wide.along(sums, bit))
        for group in groups.values():
            group.advance()
    attention, proj = groups.pop("t"), groups.pop("p")
    gate_grad, up_grad, down_grad = finish_feed(groups.values(), counts, columns)
    query_grad, key_grad, value_grad, proj_grad = finish_attention(attention, proj)

    return (
        output,
        input_grad,
        query_grad,
        key_grad,
        value_grad,
        proj_grad.T,
        gate_grad,
        up_grad,
        down_grad.T,
        sums[4],
        sums[5],
        sums[0],
        sums[1],
        sums[2],
        sums[3],
    )


def solution(mesh):
    rows = P(("wide", "narrow"), None)
    across = P(None, "narrow")
    return jax.shard_map(
        on_device,
        mesh=mesh,
        in_specs=(rows, P("wide", None))
        + (across,) * 3
        + (P("narrow", None),)
        + (across,) * 2
        + (P("narrow", None),)
        + (P(),) * 6
        + (rows,),
        out_specs=(rows, rows)
        + (P("wide", "narrow"),) * 3
        + (P("narrow", "wide"),)
        + (P("wide", "narrow"),) * 2
        + (P("narrow", "wide"),)
        + (P(),) * 6,
        check_vma=False,
    )
```
